128 devices in a mesh: patch: 16 (over z_lo, x, core), head: 8 (over z_hi, y).
Axes of the slice: x: 4, y: 4, z: 4 (z_hi: 2, z_lo: 2; z = z_hi * 2 + z_lo), core: 2. Of those that a mesh axis runs over, the one named last changes fastest.
Arguments:
- image: bfloat16 [12288, 3072], P('patch', 'head'), may hold values from -6 to 6
- text: bfloat16 [256, 3072], P(None, 'head'), may hold values from -6 to 6
- text_len: int32 [1], replicated, may hold values from 64 to 256
- img_mod: float32 [3, 3072], replicated, may hold values from -4.2 to 4.2
- txt_mod: float32 [3, 3072], replicated, may hold values from -4.2 to 4.2
- img_qkv: bfloat16 [3072, 3, 3072], P(None, None, 'head'), may hold values from -0.109375 to 0.109375
- txt_qkv: bfloat16 [3072, 3, 3072], P(None, None, 'head'), may hold values from -0.109375 to 0.109375
- img_proj: bfloat16 [3072, 3072], P('head'), may hold values from -0.109375 to 0.109375
- txt_proj: bfloat16 [3072, 3072], P('head'), may hold values from -0.109375 to 0.109375
- img_gain: float32 [2, 128], replicated, may hold values from 1 to 2.5
- txt_gain: float32 [2, 128], replicated, may hold values from 1 to 2.5
- stale_kv: bfloat16 [2, 12288, 3072], P(None, 'patch', 'head'), may hold values from -2.5 to 2.5
Outputs:
- img_out: bfloat16 [12288, 3072], P('patch', 'head')
- txt_out: bfloat16 [256, 3072], P(None, 'head')
The draws below stay inside these ranges and needn't reach their ends.
All inputs are finite; a program needn't handle non-finite values.
Results may differ from the reference program's by a relative error of at most 0.018.
Values may be sent and summed in bfloat16 or wider, within the bound.
No kernel may reach another device: no remote copies, remote signals or barrier semaphores. Data moves between devices by JAX's collectives and lax.ppermute only.
A program may use at most 128 MiB of HBM per device.

```python
import math
import jax
import jax.numpy as jnp
from jax import lax

D = 3072
HEADS = 24
HD = 128
TXT = 256
GROUP = 768
TOKENS = 12288
N_PATCH = 16
N_HEAD = 8


def block_scale(key, shape, shards, low, top_value):
    loudness = 1.0
    for position, shards_of in shards:
        draws = jax.random.uniform(jax.random.fold_in(jax.random.fold_in(key, 6), position), (shards_of,), jnp.float32, low / len(shards), top_value / len(shards))
        loudness = loudness * jnp.repeat(jnp.exp(draws), shape[position] // shards_of).reshape((-1,) + (1,) * (len(shape) - 1 - position))
    return loudness


def centred(rng, extent, scale, reach, cuts=(), kind=jnp.bfloat16):
    loudness = block_scale(rng, extent, cuts, -0.22, 0.18) if cuts else 1.0
    result = jax.random.normal(rng, extent, jnp.float32) * scale * loudness
    return jnp.minimum(jnp.maximum(result, -reach), reach).astype(kind)


def setup_inputs(seed: int = 0) -> dict:
    splits = jax.random.split(jax.random.key(seed), 13)
    return {
        "image": centred(splits[0], (TOKENS, D), 1.0, 6.0, ((0, 16), (1, 8))),
        "text": centred(splits[1], (TXT, D), 1.0, 6.0, ((1, 8),)),
        "text_len": jax.random.randint(splits[2], (1,), TXT // 4, TXT + 1).astype(jnp.int32),
        "img_mod": centred(splits[3], (3, D), 0.7, 4.2, (), jnp.float32),
        "txt_mod": centred(splits[4], (3, D), 0.7, 4.2, (), jnp.float32),
        "img_qkv": centred(splits[5], (D, 3, D), D ** -0.5, 0.109375, ((2, 8),)),
        "txt_qkv": centred(splits[6], (D, 3, D), D ** -0.5, 0.109375, ((2, 8),)),
        "img_proj": centred(splits[7], (D, D), D ** -0.5, 0.109375, ((0, 8),)),
        "txt_proj": centred(splits[8], (D, D), D ** -0.5, 0.109375, ((0, 8),)),
        "img_gain": jnp.clip(jnp.exp(jax.random.uniform(splits[9], (2, HD), jnp.float32, math.log(1.0), math.log(2.5))), 1.0, 2.5),
        "txt_gain": jnp.clip(jnp.exp(jax.random.uniform(splits[10], (2, HD), jnp.float32, math.log(1.0), math.log(2.5))), 1.0, 2.5),
        "stale_kv": jnp.clip(jax.random.uniform(splits[11], (2, TOKENS, D), jnp.float32, -2.5, 2.5) * block_scale(splits[11], (2, TOKENS, D), ((1, 16), (2, 8)), -0.4, 0.0), -2.5, 2.5).astype(jnp.bfloat16),
    }


EPS_NORM = 1e-06

def modulate(rows, mod):
    values = rows.astype(jnp.float32)
    center = values - lax.optimization_barrier(jnp.mean(values, axis=-1, keepdims=True))
    spread = lax.optimization_barrier(jnp.mean(center * center, axis=-1, keepdims=True))
    normed = center * lax.rsqrt(spread + EPS_NORM)
    return (normed * (1.0 + mod[1]) + mod[0]).astype(jnp.bfloat16)

def rms_gain(part, gain):
    return part * lax.rsqrt(lax.optimization_barrier(jnp.mean(part * part, axis=-1, keepdims=True)) + EPS_NORM) * gain

def project_heads(modded, weight, gains):
    count = modded.shape[0]
    mixed = jnp.dot(modded, weight.reshape(D, 3 * D), preferred_element_type=jnp.float32)
    mixed = mixed.reshape(count, 3, HEADS, HD)
    query = rms_gain(mixed[:, 0], gains[0]).astype(jnp.bfloat16)
    keys = rms_gain(mixed[:, 1], gains[1]).astype(jnp.bfloat16)
    return (query, keys, mixed[:, 2].astype(jnp.bfloat16))

def attend(query, keys, values, keep):
    scores = jnp.einsum('rhd,nhd->hrn', query.astype(jnp.float32), keys.astype(jnp.float32)) * HD ** (-0.5)
    weights = jnp.exp(scores) * keep
    rounded = weights.astype(jnp.bfloat16).astype(jnp.float32)
    numer = jnp.einsum('hrn,nhd->rhd', rounded, values.astype(jnp.float32))
    return (numer, lax.optimization_barrier(jnp.sum(weights, axis=2)).T)

def finish(pair):
    numer, total = pair
    out = (numer / total[:, :, None]).astype(jnp.bfloat16)
    return out.reshape(out.shape[0], D)

def project_out(rows_in, attn, proj, mod):
    count = attn.shape[0]
    pieces = attn.reshape(count, N_HEAD, D // N_HEAD).transpose(1, 0, 2)
    blocks = proj.reshape(N_HEAD, D // N_HEAD, D)

    def add_block(total, pair):
        part = jnp.dot(pair[0], pair[1], preferred_element_type=jnp.float32).astype(jnp.bfloat16)
        part = lax.optimization_barrier(part)
        return (total + part.astype(jnp.float32), None)
    total, _ = lax.scan(add_block, jnp.zeros((count, D), jnp.float32), (pieces, blocks))
    return (rows_in.astype(jnp.float32) + mod[2] * total).astype(jnp.bfloat16)

def reference(image, text, text_len, img_mod, txt_mod, img_qkv, txt_qkv, img_proj, txt_proj, img_gain, txt_gain, stale_kv):
    txt_q, txt_k, txt_v = project_heads(modulate(text, txt_mod), txt_qkv, txt_gain)
    text_keep = (jnp.arange(TXT) < text_len[0]).astype(jnp.float32)
    every_key = jnp.ones((GROUP,), jnp.float32)

    def fresh(rows):
        return project_heads(modulate(rows, img_mod), img_qkv, img_gain)
    img_q, img_k, img_v = lax.map(fresh, image.reshape(N_PATCH, GROUP, D))
    stale_k = stale_kv[0].reshape(N_PATCH, GROUP, HEADS, HD)
    stale_v = stale_kv[1].reshape(N_PATCH, GROUP, HEADS, HD)

    def image_group(index):
        query = img_q[index]

        def step(carry, other):
            keys = jnp.where(other == index, img_k[other], stale_k[other])
            values = jnp.where(other == index, img_v[other], stale_v[other])
            part = attend(query, keys, values, every_key)
            return ((carry[0] + part[0], carry[1] + part[1]), None)
        start = attend(query, txt_k, txt_v, text_keep)
        pair, _ = lax.scan(step, start, jnp.arange(N_PATCH))
        return finish(pair)
    img_attn = lax.map(image_group, jnp.arange(N_PATCH)).reshape(TOKENS, D)

    def text_step(carry, other):
        part = attend(txt_q, img_k[other], img_v[other], every_key)
        return ((carry[0] + part[0], carry[1] + part[1]), None)
    txt_pair, _ = lax.scan(text_step, attend(txt_q, txt_k, txt_v, text_keep), jnp.arange(N_PATCH))
    txt_attn = finish(txt_pair)
    img_out = project_out(image, img_attn, img_proj, img_mod)
    txt_out = project_out(text, txt_attn, txt_proj, txt_mod)
    return (img_out, txt_out)
```

```python
import functools
import math

import jax
import jax.numpy as jnp
from jax import lax
from jax.experimental import pallas as pl
from jax.experimental.pallas import tpu as pltpu
from jax.sharding import PartitionSpec as P

EPS_NORM = 1e-06
BF = jnp.bfloat16
F32 = jnp.float32
VMEM = 56 * 2**20
NX, NY = 4, 4


def patch_perm(dz, dx, dc):
    return [
        ((z * NX + x) * 2 + c, ((z ^ dz) * NX + (x + dx) % NX) * 2 + (c ^ dc))
        for z in range(2)
        for x in range(NX)
        for c in range(2)
    ]


def head_perm(dz, dy):
    return [(z * NY + y, (z ^ dz) * NY + (y + dy) % NY) for z in range(2) for y in range(NY)]


def send_patch(x, dz=0, dx=0, dc=0):
    return lax.ppermute(x, "patch", patch_perm(dz, dx, dc))


def send_head(x, dz=0, dy=0):
    return lax.ppermute(x, "head", head_perm(dz, dy))


def after(x, *deps):
    return lax.optimization_barrier((x,) + deps)[0]


def lane_sum(parts, hd):
    acc = None
    for p in parts:
        for c in range(0, p.shape[1], hd):
            piece = p[:, c : c + hd]
            acc = piece if acc is None else acc + piece
    return jnp.sum(acc, axis=-1, keepdims=True)


def qkv_kernel(idx_ref, *refs, blocks, rows, tile, scale):
    x_refs = refs[:blocks]
    wi_ref, wt_ref, mi_ref, mt_ref, gi_ref, gt_ref = refs[blocks : blocks + 6]
    q_ref, kv_ref, t_ref, x_buf, wi_buf, wt_buf, mod_buf, x_sem, wi_sem, wt_sem = refs[blocks + 6 :]
    width = x_buf.shape[2]
    total = width * blocks
    hd = gi_ref.shape[1]
    bounds = [(r, tile) for r in range(0, rows, tile)] + [(rows, x_buf.shape[1] - rows)]

    def x_copy(t, n):
        r, size = bounds[t]
        return pltpu.make_async_copy(
            x_refs[n].at[pl.ds(r, size)], x_buf.at[n, pl.ds(r, size)], x_sem.at[t, n]
        )

    def w_copy(src, dst, sem, part, n):
        start = pl.multiple_of(idx_ref[n] * width, width)
        return pltpu.make_async_copy(
            src.at[part, pl.ds(start, width)], dst.at[part, pl.ds(n * width, width)], sem.at[part, n]
        )

    def all_w(src, dst, sem):
        return [w_copy(src, dst, sem, p, n) for p in range(3) for n in range(blocks)]

    wi_all, wt_all = all_w(wi_ref, wi_buf, wi_sem), all_w(wt_ref, wt_buf, wt_sem)
    for n in range(blocks):
        x_copy(0, n).start()
    for copy in wi_all:
        copy.start()
    for t in range(1, len(bounds)):
        for n in range(blocks):
            x_copy(t, n).start()
    for copy in wt_all:
        copy.start()

    def normalise(t, mod_ref):
        r, size = bounds[t]
        for n in range(blocks):
            x_copy(t, n).wait()
        step = min(16, size)
        for o in range(r, r + size, step):
            vals = [x_buf[n, o : o + step].astype(F32) for n in range(blocks)]
            mean = lane_sum(vals, hd) * (1.0 / total)
            vals = [v - mean for v in vals]
            spread = lane_sum([v * v for v in vals], hd) * (1.0 / total)
            rstd = lax.rsqrt(spread + EPS_NORM)
            for n, v in enumerate(vals):
                m = mod_ref[idx_ref[n]]
                out = v * rstd * (1.0 + m[1:2]) + m[0:1]
                mod_buf[o : o + step, n * width : (n + 1) * width] = out.astype(BF)

    def multiply(t, w_buf, gain_ref):
        r, size = bounds[t]
        modded = mod_buf[r : r + size]
        outs = []
        for part in range(3):
            mixed = jnp.dot(modded, w_buf[part], preferred_element_type=F32)
            if part < 2:
                gain = gain_ref[part : part + 1, :] * (scale if part == 0 else 1.0)
                heads = []
                for h in range(width // hd):
                    v = mixed[:, h * hd : (h + 1) * hd]
                    rms = lax.rsqrt(jnp.mean(v * v, axis=-1, keepdims=True) + EPS_NORM)
                    heads.append(v * rms * gain)
                mixed = jnp.concatenate(heads, axis=1)
            outs.append(mixed.astype(BF))
        return outs

    normalise(0, mi_ref)
    for copy in wi_all:
        copy.wait()
    last = len(bounds) - 1
    for t in range(last):
        r, size = bounds[t]
        outs = multiply(t, wi_buf, gi_ref)
        q_ref[r : r + size] = outs[0]
        kv_ref[0, r : r + size] = outs[1]
        kv_ref[1, r : r + size] = outs[2]
        normalise(t + 1, mi_ref if t + 1 < last else mt_ref)
    for copy in wt_all:
        copy.wait()
    for p, out in enumerate(multiply(last, wt_buf, gt_ref)):
        t_ref[:, p * width : (p + 1) * width] = out


def qkv(idx, x_list, wi, wt, mod_i, mod_t, gain_i, gain_t, rows, tile):
    width = x_list[0].shape[1]
    t_rows = x_list[0].shape[0] - rows
    n = len(x_list)
    hd = gain_i.shape[1]
    depth = n * width
    scale = hd ** (-0.5) * math.log2(math.e)
    hbm = pl.BlockSpec(memory_space=pl.ANY)
    vmem = pl.BlockSpec(memory_space=pltpu.VMEM)
    tiles = rows // tile + 1
    return pl.pallas_call(
        functools.partial(qkv_kernel, blocks=n, rows=rows, tile=tile, scale=scale),
        in_specs=[pl.BlockSpec(memory_space=pltpu.SMEM)] + [hbm] * (n + 2) + [vmem] * 4,
        out_specs=[vmem] * 3,
        out_shape=[
            jax.ShapeDtypeStruct((rows, width), BF),
            jax.ShapeDtypeStruct((2, rows, width), BF),
            jax.ShapeDtypeStruct((t_rows, 3 * width), BF),
        ],
        scratch_shapes=[
            pltpu.VMEM((n, rows + t_rows, width), BF),
            pltpu.VMEM((3, depth, width), BF),
            pltpu.VMEM((3, depth, width), BF),
            pltpu.VMEM((rows + t_rows, depth), BF),
            pltpu.SemaphoreType.DMA((tiles, n)),
            pltpu.SemaphoreType.DMA((3, n)),
            pltpu.SemaphoreType.DMA((3, n)),
        ],
        compiler_params=pltpu.CompilerParams(vmem_limit_bytes=VMEM),
        cost_estimate=pl.CostEstimate(
            flops=2 * rows * depth * 3 * width, bytes_accessed=4 * depth * 3 * width, transcendentals=0
        ),
        name="qkv",
    )(idx, *x_list, wi, wt, mod_i, mod_t, gain_i, gain_t)


def one(q, k, v, valid=None):
    s = lax.dot_general(q, k, (((1,), (1,)), ((), ())), preferred_element_type=F32)
    e = jnp.exp2(s)
    if valid is not None:
        e = jnp.where(lax.broadcasted_iota(jnp.int32, e.shape, 1) < valid, e, 0.0)
    hd = v.shape[1]
    wide = jnp.concatenate([v, jnp.ones_like(v)], axis=1)
    both = jnp.dot(e.astype(BF), wide, preferred_element_type=F32)
    return both[:, :hd], both[:, hd:]


def att_kernel(*refs, plan, n_q, n_kv, text, acc, packed):
    refs = list(refs)
    length = refs.pop(0) if text else None
    qs = [refs.pop(0) for _ in range(n_q)]
    kvs = [refs.pop(0) for _ in range(n_kv)]
    txt = [refs.pop(0) for _ in range(2)] if text else None
    accs = [refs.pop(0) for _ in range(2 * n_q)] if acc else None
    for i in range(n_q):
        num = accs[2 * i][...] if acc else None
        den = accs[2 * i + 1][...] if acc else None
        q = qs[i][...]
        parts = [(kvs[j].at[0], kvs[j].at[1], None) for j in plan[i]]
        if text and i == 0:
            parts.append((txt[0], txt[1], length[0]))
        for k_ref, v_ref, valid in parts:
            n, d = one(q, k_ref[...], v_ref[...], valid)
            num = n if num is None else num + n
            den = d if den is None else den + d
        if i in packed:
            out = refs.pop(0)
            out[0] = num.astype(BF)
            out[1] = den.astype(BF)
        else:
            refs.pop(0)[...] = num
            refs.pop(0)[...] = den


def attention(qs, kvs, plan, text=None, acc=None, packed=(), name="att"):
    rows, width = qs[0].shape
    hd = 128
    heads = width // hd
    n_q, n_kv = len(qs), len(kvs)
    args, specs = [], []
    if text is not None:
        args.append(text[0])
        specs.append(pl.BlockSpec(memory_space=pltpu.SMEM))
    q_spec = pl.BlockSpec((rows, hd), lambda h: (0, h))
    for q in qs:
        args.append(q)
        specs.append(q_spec)
    for kv in kvs:
        args.append(kv)
        specs.append(pl.BlockSpec((2, kv.shape[1], hd), lambda h: (0, 0, h)))
    if text is not None:
        tk = text[1]
        args += [tk, tk]
        specs.append(pl.BlockSpec((tk.shape[0], hd), lambda h: (0, heads + h)))
        specs.append(pl.BlockSpec((tk.shape[0], hd), lambda h: (0, 2 * heads + h)))
    if acc is not None:
        args += list(acc)
        specs += [q_spec] * len(acc)
    outs, out_specs = [], []
    for i in range(n_q):
        if i in packed:
            outs.append(jax.ShapeDtypeStruct((2, rows, width), BF))
            out_specs.append(pl.BlockSpec((2, rows, hd), lambda h: (0, 0, h)))
        else:
            outs += [jax.ShapeDtypeStruct((rows, width), F32)] * 2
            out_specs += [q_spec] * 2
    blocks = sum(len(p) for p in plan)
    keys = kvs[0].shape[1]
    return pl.pallas_call(
        functools.partial(
            att_kernel, plan=plan, n_q=n_q, n_kv=n_kv, text=text is not None, acc=acc is not None, packed=packed
        ),
        grid=(heads,),
        in_specs=specs,
        out_specs=out_specs,
        out_shape=outs,
        compiler_params=pltpu.CompilerParams(vmem_limit_bytes=VMEM),
        cost_estimate=pl.CostEstimate(
            flops=8 * rows * keys * width * blocks,
            bytes_accessed=4 * width * keys * n_kv,
            transcendentals=rows * keys * heads * blocks,
        ),
        name=name,
    )(*args)


def text_kernel(len_ref, got_ref, q_ref, txt_ref, proj_ref, out_ref):
    width = q_ref.shape[1]
    hd = 128
    parts = []
    for h in range(width // hd):
        cols = slice(h * hd, (h + 1) * hd)
        k = txt_ref[:, width + h * hd : width + (h + 1) * hd]
        v = txt_ref[:, 2 * width + h * hd : 2 * width + (h + 1) * hd]
        n, d = one(q_ref[:, cols], k, v, len_ref[0])
        num = n + jnp.sum(got_ref[:, 0, :, cols].astype(F32), axis=0)
        den = d + jnp.sum(got_ref[:, 1, :, cols].astype(F32), axis=0)
        parts.append((num / den).astype(BF))
    attn = jnp.concatenate(parts, axis=1)
    part = jnp.dot(attn, proj_ref[...], preferred_element_type=F32).astype(BF)
    for j in range(out_ref.shape[0]):
        out_ref[j] = part[:, j * width : (j + 1) * width]


def text_finish(text_len, got, q, txt, proj, n_head):
    rows, width = q.shape
    return pl.pallas_call(
        text_kernel,
        in_specs=[pl.BlockSpec(memory_space=pltpu.SMEM)] + [pl.BlockSpec(memory_space=pltpu.VMEM)] * 4,
        out_specs=pl.BlockSpec(memory_space=pltpu.VMEM),
        out_shape=jax.ShapeDtypeStruct((n_head, rows, width), BF),
        compiler_params=pltpu.CompilerParams(vmem_limit_bytes=VMEM),
        name="text_finish",
    )(text_len, got, q, txt, proj)


def quotient_kernel(zh_ref, num_ref, den_ref, got_ref, out_ref):
    hd = 128
    for h in range(num_ref.shape[1] // hd):
        cols = slice(h * hd, (h + 1) * hd)
        num = num_ref[:, cols] + got_ref[0, :, cols].astype(F32)
        den = den_ref[:, cols] + got_ref[1, :, cols].astype(F32)
        out_ref[:, cols] = (num / den).astype(BF)


def quotient(zh, num, den, got):
    rows, width = num.shape
    half = rows // 2

    def pick(i, zh_ref):
        return (lax.rem(i + zh_ref[0], 2), 0)

    return pl.pallas_call(
        quotient_kernel,
        grid_spec=pltpu.PrefetchScalarGridSpec(
            num_scalar_prefetch=1,
            grid=(2,),
            in_specs=[
                pl.BlockSpec((half, width), pick),
                pl.BlockSpec((half, width), pick),
                pl.BlockSpec((2, half, width), lambda i, s: (0,) + pick(i, s)),
            ],
            out_specs=pl.BlockSpec((None, half, width), lambda i, s: (i, 0, 0)),
        ),
        out_shape=jax.ShapeDtypeStruct((2, half, width), BF),
        compiler_params=pltpu.CompilerParams(vmem_limit_bytes=VMEM),
        name="quotient",
    )(zh, num, den, got)


def proj_kernel(pos_ref, mine_ref, got_ref, w_ref, wz_ref, *outs):
    width = mine_ref.shape[1]
    zh, y = pos_ref[0], pos_ref[1]
    rows = jnp.concatenate([mine_ref[...], got_ref[...]], axis=1)
    for d, out in enumerate(outs):
        for s in range(2):
            block = lax.rem(zh + s, 2) * NY + lax.rem(y + d, NY)
            cols = pl.ds(pl.multiple_of(block * width, 128), width)
            w = jnp.concatenate([w_ref[:, cols], wz_ref[:, cols]], axis=0)
            out[s] = jnp.dot(rows, w, preferred_element_type=F32).astype(BF)


def project(pos, mine, got, w, wz):
    rows, width = mine.shape
    spec = pl.BlockSpec(memory_space=pltpu.VMEM)
    return pl.pallas_call(
        proj_kernel,
        in_specs=[pl.BlockSpec(memory_space=pltpu.SMEM)] + [spec] * 4,
        out_specs=[spec] * NY,
        out_shape=[jax.ShapeDtypeStruct((2, rows, width), BF)] * NY,
        compiler_params=pltpu.CompilerParams(vmem_limit_bytes=VMEM),
        name="project",
    )(pos, mine, got, w, wz)


def shards(
    image,
    text,
    text_len,
    img_mod,
    txt_mod,
    img_qkv,
    txt_qkv,
    img_proj,
    txt_proj,
    img_gain,
    txt_gain,
    stale_kv,
):
    n_head = lax.axis_size("head")
    n_patch = lax.axis_size("patch")
    me_h = lax.axis_index("head")
    me_p = lax.axis_index("patch")
    zh, y = me_h // NY, me_h % NY
    group, width = image.shape
    txt_total = text.shape[0]
    t_rows = txt_total // n_patch

    t_own = lax.dynamic_slice_in_dim(text, me_p * t_rows, t_rows, 0)
    rows = jnp.concatenate([image, t_own], axis=0)
    i_z = send_head(rows, dz=1)
    i_m = send_head(rows, dy=1)
    i_p = send_head(rows, dy=-1)
    kv_z = send_patch(stale_kv, dz=1)
    kv_m = send_patch(stale_kv, dx=1)
    i_2 = send_head(i_m, dy=1)
    iz_p = send_head(i_z, dy=-1)
    kv_p = send_patch(after(stale_kv, i_z), dx=-1)
    iz_m = send_head(after(i_z, i_2), dy=1)
    iz_2 = send_head(iz_p, dy=-1)
    kv_2 = send_patch(after(kv_m, i_2), dx=1)
    kvz_p = send_patch(after(kv_z, kv_p), dx=-1)
    kvz_m = send_patch(after(kv_z, kv_2), dx=1)
    kvz_2 = send_patch(kvz_p, dx=-1)
    proj_z = send_head(after(img_proj, kv_z), dz=1)

    mod_i = img_mod.reshape(3, n_head, width).transpose(1, 0, 2)
    mod_t = txt_mod.reshape(3, n_head, width).transpose(1, 0, 2)
    w_i = img_qkv.transpose(1, 0, 2)
    w_t = txt_qkv.transpose(1, 0, 2)
    ring = (y + jnp.array([0, 0, NY - 1, NY - 1, 1, 1, 2, 2])) % NY
    side = (zh + jnp.array([0, 1] * 4)) % 2
    idx = (side * NY + ring).astype(jnp.int32)
    q, kv, t_pack = qkv(
        idx, [rows, i_z, i_m, iz_m, i_p, iz_p, i_2, iz_2], w_i, w_t, mod_i, mod_t, img_gain, txt_gain, group, group // 3
    )
    q_c = send_patch(q, dc=1)
    t_q = t_pack[:, :width]
    txt = lax.all_to_all(
        jnp.broadcast_to(t_pack[None], (n_patch,) + t_pack.shape), "patch", 0, 0
    ).reshape(txt_total, 3 * width)

    num, den = attention([q], [kv, kv_m, kv_p, kv_z], [[0, 1, 2, 3]], name="att_own")
    num_c, den_c = attention([q_c], [stale_kv, kv_m, kv_p, kv_z], [[0, 1, 2, 3]], name="att_swap")
    both = attention([q, q_c], [kv_2, kvz_p], [[0, 1], [0, 1]], acc=(num, den, num_c, den_c), name="att_mid")
    num, den, part_c = attention(
        [q, q_c], [kvz_m, kvz_2], [[0, 1], [0, 1]], text=(text_len, txt), acc=both, packed=(1,), name="att_last"
    )
    got_c = send_patch(part_c, dc=1)

    t_all = txt[:, :width]
    (t_part,) = attention([t_all], [kv], [[0]], packed=(0,), name="att_text")
    t_part = t_part.reshape(2, n_patch, t_rows, width).transpose(1, 0, 2, 3)
    t_got = lax.all_to_all(t_part, "patch", 0, 0)
    t_proj = text_finish(text_len, t_got, t_q, txt, txt_proj, n_head)
    t_sum = lax.all_to_all(t_proj, "head", 0, 0).astype(F32).sum(axis=0)
    column = me_h * width
    txt_gate = lax.dynamic_slice_in_dim(txt_mod[2], column, width)
    t_out = (t_own.astype(F32) + txt_gate * t_sum).astype(BF)
    txt_out = lax.all_to_all(
        jnp.broadcast_to(t_out[None], (n_patch,) + t_out.shape), "patch", 0, 0
    ).reshape(txt_total, width)

    zh1 = zh.astype(jnp.int32).reshape(1)
    halves = quotient(zh1, num, den, got_c)
    from_z = send_head(halves[1], dz=1)
    pos = jnp.stack([zh, y]).astype(jnp.int32)
    p0, p1, p2, p3 = project(pos, halves[0], from_z, img_proj, proj_z)
    r1 = send_head(p1, dy=1)
    r2 = send_head(p2, dy=2)
    r3 = send_head(p3, dy=3)
    total = p0.astype(F32) + r1.astype(F32) + r2.astype(F32) + r3.astype(F32)
    mine = total[0].astype(BF)
    other = send_head(total[1].astype(BF), dz=1)
    top = jnp.where(zh == 0, mine, other)
    low = jnp.where(zh == 0, other, mine)
    img_sum = jnp.concatenate([top, low], axis=0).astype(F32)
    img_gate = lax.dynamic_slice_in_dim(img_mod[2], column, width)
    img_out = (image.astype(F32) + img_gate * img_sum).astype(BF)
    return (img_out, txt_out)


def solution(mesh):
    in_specs = (
        P("patch", "head"),
        P(None, "head"),
        P(),
        P(),
        P(),
        P(None, None, "head"),
        P(None, None, "head"),
        P("head", None),
        P("head", None),
        P(),
        P(),
        P(None, "patch", "head"),
    )
    out_specs = (P("patch", "head"), P(None, "head"))
    return jax.shard_map(shards, mesh=mesh, in_specs=in_specs, out_specs=out_specs, check_vma=False)
```

```python
import functools
import math

import jax
import jax.numpy as jnp
from jax import lax
from jax.experimental import pallas as pl
from jax.experimental.pallas import tpu as pltpu
from jax.sharding import PartitionSpec as P

EPS_NORM = 1e-06
BF = jnp.bfloat16
F32 = jnp.float32
VMEM = 56 * 2**20
NX, NY = 4, 4
TINY = pl.CostEstimate(flops=1, bytes_accessed=1, transcendentals=0)


def cost(us):
    return pl.CostEstimate(flops=int(us * 1.15e9), bytes_accessed=1, transcendentals=0)


def patch_perm(dz, dx, dc):
    return [
        ((z * NX + x) * 2 + c, ((z ^ dz) * NX + (x + dx) % NX) * 2 + (c ^ dc))
        for z in range(2)
        for x in range(NX)
        for c in range(2)
    ]


def head_perm(dz, dy):
    return [(z * NY + y, (z ^ dz) * NY + (y + dy) % NY) for z in range(2) for y in range(NY)]


def send_patch(x, dz=0, dx=0, dc=0):
    return lax.ppermute(x, "patch", patch_perm(dz, dx, dc))


def send_head(x, dz=0, dy=0):
    return lax.ppermute(x, "head", head_perm(dz, dy))


def in_hbm(x):
    return pltpu.with_memory_space_constraint(x, pltpu.HBM)


def after(x, *deps):
    return lax.optimization_barrier((x,) + deps)[0]


def lane_sum(parts, hd):
    acc = None
    for p in parts:
        for c in range(0, p.shape[1], hd):
            piece = p[:, c : c + hd]
            acc = piece if acc is None else acc + piece
    return jnp.sum(acc, axis=-1, keepdims=True)


def moments(vals, hd):
    mean = lane_sum(vals, hd) * (1.0 / sum(v.shape[1] for v in vals))
    vals = [v - mean for v in vals]
    return mean, vals, lane_sum([v * v for v in vals], hd)


def rms_heads(mixed, gain):
    hd = gain.shape[1]
    heads = []
    for c in range(0, mixed.shape[1], hd):
        v = mixed[:, c : c + hd]
        rms = lax.rsqrt(jnp.mean(v * v, axis=-1, keepdims=True) + EPS_NORM)
        heads.append((v * rms * gain).astype(BF))
    return jnp.concatenate(heads, axis=1)


def query_scale(hd):
    return hd ** (-0.5) * math.log2(math.e)


def weight_copies(idx_ref, w_ref, w_buf, sem, first):
    width = w_ref.shape[2]
    return [
        pltpu.make_async_copy(
            w_ref.at[p, pl.ds(pl.multiple_of(idx_ref[first + n] * width, width), width)],
            w_buf.at[pl.ds(n * width, width), pl.ds(p * width, width)],
            sem.at[p, n],
        )
        for n in range(sem.shape[1])
        for p in range(3)
    ]


def early_kernel(idx_ref, *refs, blocks, rows):
    x_refs = refs[:blocks]
    w_ref, mod_ref, acc_ref, stat_ref, x_buf, w_buf, mod_buf, x_sem, w_sem = refs[blocks:]
    width = x_buf.shape[2]
    hd = stat_ref.shape[2]
    x_copies = [
        pltpu.make_async_copy(x_refs[n].at[pl.ds(0, rows)], x_buf.at[n], x_sem.at[n]) for n in range(blocks)
    ]
    w_copies = weight_copies(idx_ref, w_ref, w_buf, w_sem, 0)
    for copy in x_copies + w_copies:
        copy.start()
    for n in range(blocks):
        cols = slice(n * width, (n + 1) * width)
        m = mod_ref[idx_ref[n]]
        scale, shift = 1.0 + m[1:2], m[0:1]
        high, low = [v.astype(BF) for v in (scale, shift)]
        pieces = [high, (scale - high.astype(F32)).astype(BF), low, (shift - low.astype(F32)).astype(BF)]
        tail = mod_buf.shape[0] - rows - len(pieces)
        mod_buf[rows:, cols] = jnp.concatenate(pieces + [jnp.zeros((tail, width), BF)], axis=0)
    for copy in x_copies:
        copy.wait()
    for o in range(0, rows, 16):
        mean, vals, square = moments([x_buf[n, o : o + 16].astype(F32) for n in range(blocks)], hd)
        inverse = lax.rsqrt(square * (1.0 / (blocks * width)) + EPS_NORM)
        stat_ref[0, o : o + 16] = jnp.broadcast_to(mean, (16, hd))
        stat_ref[1, o : o + 16] = jnp.broadcast_to(square, (16, hd))
        for n, v in enumerate(vals):
            out = v * inverse * (1.0 + mod_ref[idx_ref[n]][1:2])
            mod_buf[o : o + 16, n * width : (n + 1) * width] = out.astype(BF)
    for copy in w_copies:
        copy.wait()
    acc_ref[...] = jnp.dot(mod_buf[...], w_buf[...], preferred_element_type=F32)


def late_kernel(idx_ref, *refs, first, tile, scale):
    lone = len(refs) - 15
    x_refs = list(refs[:lone]) + [refs[lone].at[0], refs[lone].at[1]]
    w_ref, acc_hbm, stat_ref, mod_ref, gain_ref, q_ref, kv_ref = refs[lone + 1 : lone + 8]
    x_buf, w_buf, acc_ref, mod_buf, x_sem, w_sem, acc_sem = refs[lone + 8 :]
    blocks, rows, width = x_buf.shape
    hd = gain_ref.shape[1]
    tiles = rows // tile
    n_first, n_last = first * width, blocks * width
    x_copies = [
        [
            pltpu.make_async_copy(
                x_refs[n].at[pl.ds(t * tile, tile)], x_buf.at[n, pl.ds(t * tile, tile)], x_sem.at[t, n]
            )
            for n in range(blocks)
        ]
        for t in range(tiles)
    ]
    w_copies = weight_copies(idx_ref, w_ref, w_buf, w_sem, first)
    acc_copy = pltpu.make_async_copy(acc_hbm, acc_ref, acc_sem)
    for copy in x_copies[0] + w_copies + [acc_copy] + sum(x_copies[1:], []):
        copy.start()
    factors = {}

    def normalise(t):
        for copy in x_copies[t]:
            copy.wait()
        ratios, shifts = [], []
        for o in range(t * tile, (t + 1) * tile, 16):
            mean, vals, square = moments([x_buf[n, o : o + 16].astype(F32) for n in range(blocks)], hd)
            mean0 = stat_ref[0, o : o + 16, 0:1]
            square0 = stat_ref[1, o : o + 16, 0:1]
            gap = mean0 - mean
            total = square + square0 + gap * gap * (n_first * n_last / (n_first + n_last))
            inverse = lax.rsqrt(total * (1.0 / (n_first + n_last)) + EPS_NORM)
            center = mean + gap * (n_first / (n_first + n_last))
            ratios.append(inverse * jnp.sqrt(square0 * (1.0 / n_first) + EPS_NORM))
            shifts.append((mean0 - center) * inverse)
            for n, v in enumerate(vals):
                m = mod_ref[idx_ref[first + n]]
                out = (v + (mean - center)) * inverse * (1.0 + m[1:2]) + m[0:1]
                mod_buf[o : o + 16, n * width : (n + 1) * width] = out.astype(BF)
        factors[t] = (jnp.concatenate(ratios, axis=0), jnp.concatenate(shifts, axis=0))

    normalise(0)
    for copy in w_copies + [acc_copy]:
        copy.wait()
    scales = acc_ref[rows : rows + 1] + acc_ref[rows + 1 : rows + 2]
    offset = acc_ref[rows + 2 : rows + 3] + acc_ref[rows + 3 : rows + 4]
    for t in range(tiles):
        part = slice(t * tile, (t + 1) * tile)
        mixed = jnp.dot(mod_buf[part], w_buf[...], preferred_element_type=F32)
        if t + 1 < tiles:
            normalise(t + 1)
        ratio, shift = factors[t]
        mixed = mixed + acc_ref[part] * ratio + shift * scales + offset
        q_ref[part] = rms_heads(mixed[:, :width], gain_ref[0:1] * scale)
        kv_ref[0, part] = rms_heads(mixed[:, width : 2 * width], gain_ref[1:2])
        kv_ref[1, part] = mixed[:, 2 * width :].astype(BF)


def early_qkv(idx, x_list, w, mod, rows):
    width = x_list[0].shape[1]
    n = len(x_list)
    hd = 128
    hbm = pl.BlockSpec(memory_space=pltpu.HBM)
    vmem = pl.BlockSpec(memory_space=pltpu.VMEM)
    return pl.pallas_call(
        functools.partial(early_kernel, blocks=n, rows=rows),
        in_specs=[pl.BlockSpec(memory_space=pltpu.SMEM)] + [hbm] * (n + 1) + [vmem],
        out_specs=[vmem] * 2,
        out_shape=[
            jax.ShapeDtypeStruct((rows + 16, 3 * width), F32),
            jax.ShapeDtypeStruct((2, rows, hd), F32),
        ],
        scratch_shapes=[
            pltpu.VMEM((n, rows, width), BF),
            pltpu.VMEM((n * width, 3 * width), BF),
            pltpu.VMEM((rows + 16, n * width), BF),
            pltpu.SemaphoreType.DMA((n,)),
            pltpu.SemaphoreType.DMA((3, n)),
        ],
        compiler_params=pltpu.CompilerParams(vmem_limit_bytes=VMEM),
        cost_estimate=TINY,
        name="early_qkv",
    )(idx, *x_list, w, mod)


def late_qkv(idx, x_list, w, acc, stat, mod, gain):
    rows, width = stat.shape[1], x_list[0].shape[1]
    n = len(x_list) + 1
    first = mod.shape[0] - n
    tile = rows // 2
    hbm = pl.BlockSpec(memory_space=pltpu.HBM)
    vmem = pl.BlockSpec(memory_space=pltpu.VMEM)
    return pl.pallas_call(
        functools.partial(
            late_kernel, first=first, tile=tile, scale=query_scale(gain.shape[1])
        ),
        in_specs=[pl.BlockSpec(memory_space=pltpu.SMEM)] + [hbm] * (n + 1) + [vmem] * 3,
        out_specs=[vmem] * 2,
        out_shape=[
            jax.ShapeDtypeStruct((rows, width), BF),
            jax.ShapeDtypeStruct((2, rows, width), BF),
        ],
        scratch_shapes=[
            pltpu.VMEM((n, rows, width), BF),
            pltpu.VMEM((n * width, 3 * width), BF),
            pltpu.VMEM(acc.shape, F32),
            pltpu.VMEM((rows, n * width), BF),
            pltpu.SemaphoreType.DMA((2, n)),
            pltpu.SemaphoreType.DMA((3, n)),
            pltpu.SemaphoreType.DMA,
        ],
        compiler_params=pltpu.CompilerParams(vmem_limit_bytes=VMEM),
        cost_estimate=TINY,
        name="late_qkv",
    )(idx, *x_list, w, acc, stat, mod, gain)


def text_qkv_kernel(idx_ref, *refs, blocks, scale):
    x_refs = list(refs[: blocks - 2]) + [refs[blocks - 2].at[0], refs[blocks - 2].at[1]]
    w_ref, mod_ref, gain_ref, out_ref, mod_buf = refs[blocks - 1 :]
    width = x_refs[0].shape[1]
    vals = [r[...].astype(F32) for r in x_refs]
    _, vals, square = moments(vals, gain_ref.shape[1])
    inverse = lax.rsqrt(square * (1.0 / (blocks * width)) + EPS_NORM)
    for n, v in enumerate(vals):
        m = mod_ref[idx_ref[n]]
        out = (v * inverse * (1.0 + m[1:2]) + m[0:1]).astype(BF)
        mod_buf[:, pl.ds(pl.multiple_of(idx_ref[n] * width, 128), width)] = out
    mixed = [jnp.dot(mod_buf[...], w_ref[p], preferred_element_type=F32) for p in range(3)]
    out_ref[:, :width] = rms_heads(mixed[0], gain_ref[0:1] * scale)
    out_ref[:, width : 2 * width] = rms_heads(mixed[1], gain_ref[1:2])
    out_ref[:, 2 * width :] = mixed[2].astype(BF)


def text_qkv(idx, x_list, w, mod, gain, rows):
    total, width = x_list[0].shape
    n = len(x_list) + 1
    last = total // rows - 1
    vmem = pl.BlockSpec(memory_space=pltpu.VMEM)
    return pl.pallas_call(
        functools.partial(text_qkv_kernel, blocks=n, scale=query_scale(gain.shape[1])),
        grid=(1,),
        in_specs=[pl.BlockSpec(memory_space=pltpu.SMEM)]
        + [pl.BlockSpec((rows, width), lambda i: (last, 0))] * (n - 2)
        + [pl.BlockSpec((2, rows, width), lambda i: (0, last, 0))]
        + [vmem] * 3,
        out_specs=vmem,
        out_shape=jax.ShapeDtypeStruct((rows, 3 * width), BF),
        scratch_shapes=[pltpu.VMEM((rows, n * width), BF)],
        compiler_params=pltpu.CompilerParams(vmem_limit_bytes=24 * 2**20),
        cost_estimate=cost(2),
        name="text_qkv",
    )(idx, *[in_hbm(x) for x in x_list], w, mod, gain)


def one(q, k, v, valid=None):
    s = lax.dot_general(q, k, (((1,), (1,)), ((), ())), preferred_element_type=F32)
    e = jnp.exp2(s)
    if valid is not None:
        e = jnp.where(lax.broadcasted_iota(jnp.int32, e.shape, 1) < valid, e, 0.0)
    hd = v.shape[1]
    wide = jnp.concatenate([v, jnp.ones_like(v)], axis=1)
    both = jnp.dot(e.astype(BF), wide, preferred_element_type=F32)
    return both[:, :hd], both[:, hd:]


def att_kernel(pos_ref, *refs, plan, n_q, n_kv, text, acc, packed):
    refs = list(refs)
    length = refs.pop(0) if text else None
    qs = [refs.pop(0) for _ in range(n_q)]
    kvs = [refs.pop(0) for _ in range(n_kv)]
    txt = [refs.pop(0) for _ in range(2)] if text else None
    accs = [refs.pop(0) for _ in range(2 * n_q)] if acc else None
    for i in range(n_q):
        num = accs[2 * i][...] if acc else None
        den = accs[2 * i + 1][...] if acc else None
        q = qs[i][...]
        parts = [(kvs[j].at[0], kvs[j].at[1], None) for j in plan[i]]
        if text and i == 0:
            parts.append((txt[0], txt[1], length[0]))
        for k_ref, v_ref, valid in parts:
            n, d = one(q, k_ref[...], v_ref[...], valid)
            num = n if num is None else num + n
            den = d if den is None else den + d
        if i in packed:
            out = refs.pop(0)
            out[0] = num.astype(BF)
            out[1] = den.astype(BF)
        else:
            refs.pop(0)[...] = num
            refs.pop(0)[...] = den


def attention(pos, qs, kvs, plan, text=None, acc=None, packed=(), rows=None, chunk=0, width=None, name="att"):
    width = qs[0].shape[1] if width is None else width
    rows = qs[0].shape[0] if rows is None else rows
    hd = 128
    heads = width // hd
    n_q = len(qs)
    args, specs = [], []
    if text is not None:
        args.append(text[0])
        specs.append(pl.BlockSpec(memory_space=pltpu.SMEM))
    q_spec = pl.BlockSpec((rows, hd), lambda h, p: (chunk, h))
    out_spec = pl.BlockSpec((rows, hd), lambda h, p: (0, h))
    for q in qs:
        args.append(q)
        specs.append(q_spec)
    keys = 0
    for kv in kvs:
        keys = kv.shape[1]
        specs.append(pl.BlockSpec((2, keys, hd), lambda h, p: (0, 0, h)))
        args.append(kv)
    if text is not None:
        tk = text[1]
        args += [tk, tk]
        specs.append(pl.BlockSpec((tk.shape[0], hd), lambda h, p: (0, heads + h)))
        specs.append(pl.BlockSpec((tk.shape[0], hd), lambda h, p: (0, 2 * heads + h)))
    if acc is not None:
        args += list(acc)
        specs += [q_spec] * len(acc)
    outs, out_specs = [], []
    for i in range(n_q):
        if i in packed:
            outs.append(jax.ShapeDtypeStruct((2, rows, width), BF))
            out_specs.append(pl.BlockSpec((2, rows, hd), lambda h, p: (0, 0, h)))
        else:
            outs += [jax.ShapeDtypeStruct((rows, width), F32)] * 2
            out_specs += [out_spec] * 2
    blocks = sum(len(p) for p in plan)
    return pl.pallas_call(
        functools.partial(
            att_kernel, plan=plan, n_q=n_q, n_kv=len(kvs), text=text is not None, acc=acc is not None, packed=packed
        ),
        grid_spec=pltpu.PrefetchScalarGridSpec(
            num_scalar_prefetch=1, grid=(heads,), in_specs=specs, out_specs=out_specs
        ),
        out_shape=outs,
        compiler_params=pltpu.CompilerParams(vmem_limit_bytes=VMEM),
        cost_estimate=pl.CostEstimate(
            flops=14 * rows * keys * width * blocks, bytes_accessed=1, transcendentals=0
        ),
        name=name,
    )(pos, *args)


def text_att_kernel(q_ref, kv_ref, out_ref):
    n_patch, _, rows, width = out_ref.shape
    hd = 128
    for h in range(width // hd):
        cols = slice(h * hd, (h + 1) * hd)
        num, den = one(q_ref[:, cols], kv_ref[0, :, cols], kv_ref[1, :, cols])
        out_ref[:, 0, :, cols] = num.astype(BF).reshape(n_patch, rows, hd)
        out_ref[:, 1, :, cols] = den.astype(BF).reshape(n_patch, rows, hd)


def text_attention(txt, kv, n_patch):
    rows = txt.shape[0]
    width = kv.shape[2]
    return pl.pallas_call(
        text_att_kernel,
        grid=(1,),
        in_specs=[pl.BlockSpec((rows, width), lambda i: (0, 0)), pl.BlockSpec(kv.shape, lambda i: (0, 0, 0))],
        out_specs=pl.BlockSpec((n_patch, 2, rows // n_patch, width), lambda i: (0, 0, 0, 0)),
        out_shape=jax.ShapeDtypeStruct((n_patch, 2, rows // n_patch, width), BF),
        compiler_params=pltpu.CompilerParams(vmem_limit_bytes=VMEM),
        cost_estimate=cost(3),
        name="text_attention",
    )(txt, kv)


def text_keys(q_ref, txt_ref, len_ref, h):
    hd = 128
    width = q_ref.shape[1]
    at = h * hd
    k = txt_ref[:, width + at : width + at + hd]
    v = txt_ref[:, 2 * width + at : 2 * width + at + hd]
    return one(q_ref[:, at : at + hd], k, v, len_ref[0])


def image_quotient(len_ref, q_ref, txt_ref, num_ref, den_ref, got_ref, attn_ref):
    hd = 128
    rows = num_ref.shape[0]
    for h in range(num_ref.shape[1] // hd):
        cols = slice(h * hd, (h + 1) * hd)
        n, d = text_keys(q_ref, txt_ref, len_ref, h)
        num = n + num_ref[:, cols] + got_ref[0, :, cols].astype(F32)
        den = d + den_ref[:, cols] + got_ref[1, :, cols].astype(F32)
        attn_ref[0:rows, cols] = (num / den).astype(BF)


def quotient(text_len, q, txt, num, den, got):
    vmem = pl.BlockSpec(memory_space=pltpu.VMEM)
    return pl.pallas_call(
        image_quotient,
        in_specs=[pl.BlockSpec(memory_space=pltpu.SMEM)] + [vmem] * 5,
        out_specs=vmem,
        out_shape=jax.ShapeDtypeStruct(q.shape, BF),
        compiler_params=pltpu.CompilerParams(vmem_limit_bytes=VMEM),
        cost_estimate=cost(4),
        name="quotient",
    )(text_len, q, txt, num, den, got)


def text_quotient_kernel(len_ref, sum_ref, q_ref, txt_ref, proj_ref, out_ref):
    rows, width = q_ref.shape
    hd = 128
    parts = []
    for h in range(width // hd):
        cols = slice(h * hd, (h + 1) * hd)
        n, d = text_keys(q_ref, txt_ref, len_ref, h)
        num = n + jnp.sum(sum_ref[:, 0, :, cols].astype(F32), axis=0)
        den = d + jnp.sum(sum_ref[:, 1, :, cols].astype(F32), axis=0)
        parts.append((num / den).astype(BF))
    attn = jnp.concatenate(parts, axis=1)
    part = jnp.dot(attn, proj_ref[...], preferred_element_type=F32).astype(BF)
    for j in range(out_ref.shape[0]):
        out_ref[j] = part[:, j * width : (j + 1) * width]


def text_quotient(text_len, sums, q, txt, proj, n_head):
    vmem = pl.BlockSpec(memory_space=pltpu.VMEM)
    return pl.pallas_call(
        text_quotient_kernel,
        in_specs=[pl.BlockSpec(memory_space=pltpu.SMEM)] + [vmem] * 4,
        out_specs=vmem,
        out_shape=jax.ShapeDtypeStruct((n_head,) + q.shape, BF),
        compiler_params=pltpu.CompilerParams(vmem_limit_bytes=VMEM),
        cost_estimate=cost(4),
        name="text_quotient",
    )(text_len, sums, q, txt, proj)


def proj_kernel(pos_ref, mine_ref, got_ref, w_ref, wz_ref, *refs):
    outs = refs[:NY]
    w_buf, sem = refs[NY:]
    width = mine_ref.shape[1]
    zh, y = pos_ref[0], pos_ref[1]
    order = (2, 1, 3, 0)

    def copies(d):
        block = lax.rem(y + d, NY)
        pairs = ((w_ref, zh * NY + block), (wz_ref, block))
        return [
            pltpu.make_async_copy(
                ref.at[:, pl.ds(pl.multiple_of(at * width, 128), width)],
                w_buf.at[d, pl.ds(i * width, width)],
                sem.at[d, i],
            )
            for i, (ref, at) in enumerate(pairs)
        ]

    for d in order:
        for copy in copies(d):
            copy.start()
    both = jnp.concatenate([mine_ref[...], got_ref[...]], axis=1)
    for d in order:
        for copy in copies(d):
            copy.wait()
        outs[d][...] = jnp.dot(both, w_buf[d], preferred_element_type=F32).astype(BF)


def project(pos, mine, got, w, wz):
    width = mine.shape[1]
    spec = pl.BlockSpec(memory_space=pltpu.VMEM)
    hbm = pl.BlockSpec(memory_space=pltpu.HBM)
    return pl.pallas_call(
        proj_kernel,
        in_specs=[pl.BlockSpec(memory_space=pltpu.SMEM)] + [spec] * 2 + [hbm] * 2,
        out_specs=[spec] * NY,
        out_shape=[jax.ShapeDtypeStruct(mine.shape, BF)] * NY,
        scratch_shapes=[
            pltpu.VMEM((NY, 2 * width, width), BF),
            pltpu.SemaphoreType.DMA((NY, 2)),
        ],
        compiler_params=pltpu.CompilerParams(vmem_limit_bytes=VMEM),
        cost_estimate=cost(6),
        name="project",
    )(pos, mine, got, w, wz)


def exchange(parts):
    total = parts[0].astype(F32)
    for d in range(1, NY):
        total = total + send_head(parts[d], dy=d).astype(F32)
    return total


def shards(
    image,
    text,
    text_len,
    img_mod,
    txt_mod,
    img_qkv,
    txt_qkv,
    img_proj,
    txt_proj,
    img_gain,
    txt_gain,
    stale_kv,
):
    n_head = lax.axis_size("head")
    n_patch = lax.axis_size("patch")
    me_h = lax.axis_index("head")
    me_p = lax.axis_index("patch")
    zh, y = me_h // NY, me_h % NY
    group, width = image.shape
    txt_total = text.shape[0]
    t_rows = txt_total // n_patch

    pos = jnp.stack([zh, y]).astype(jnp.int32)

    t_own = lax.dynamic_slice_in_dim(text, me_p * t_rows, t_rows, 0)
    rows = jnp.concatenate([image, t_own], axis=0)
    i_z = send_head(rows, dz=1)
    i_m = send_head(rows, dy=1)
    i_p = send_head(rows, dy=-1)
    kv_m = send_patch(stale_kv, dx=1)
    part_z = lax.dynamic_slice_in_dim(img_proj, (1 - zh) * NY * width, NY * width, 1)
    near = after(i_z, i_m, i_p, part_z)
    ahead = send_head(jnp.stack([i_m, near]), dy=1)
    iz_p = send_head(near, dy=-1)
    mod_i = img_mod.reshape(3, n_head, width).transpose(1, 0, 2)
    mod_t = txt_mod.reshape(3, n_head, width).transpose(1, 0, 2)
    ring = (y + jnp.array([0, 0, NY - 1, 1, 1, 2, 2, NY - 1])) % NY
    side = (zh + jnp.array([0, 1, 0, 0, 1, 1, 0, 1])) % 2
    idx = (side * NY + ring).astype(jnp.int32)
    w_i = img_qkv.transpose(1, 0, 2)
    iz_2 = send_head(iz_p, dy=-1)
    acc, stat = early_qkv(after(idx, kv_m, iz_p), [rows, near, i_m, i_p], w_i, mod_i, group)
    later = after(stale_kv, iz_p)
    kv_z = send_patch(later, dz=1)
    kv_p = send_patch(later, dx=-1)
    kv_2 = send_patch(kv_m, dx=1)
    kvz_m = send_patch(kv_z, dx=1)
    kvz_p = send_patch(kv_z, dx=-1)
    kvz_2 = send_patch(kv_2, dz=1)
    proj_z = send_head(after(part_z, kv_z), dz=1)
    q, kv = late_qkv(idx, [iz_p, iz_2, ahead], w_i, acc, stat, mod_i, img_gain)
    x_list = [rows, near, i_m, i_p, iz_p, iz_2, ahead]
    q_c = send_patch(q, dc=1)
    t_pack = text_qkv(after(idx, q), x_list, txt_qkv.transpose(1, 0, 2), mod_t, txt_gain, t_rows)
    t_q = t_pack[:, :width]
    txt = lax.all_to_all(
        jnp.broadcast_to(t_pack[None], (n_patch,) + t_pack.shape), "patch", 0, 0
    ).reshape(txt_total, 3 * width)

    both = attention(
        after(pos, t_pack), [q, q_c], [kv, stale_kv, kv_m, kv_p], [[0, 2, 3], [1, 2, 3]], name="att_near"
    )
    both = attention(pos, [q, q_c], [kv_2, kv_z], [[0, 1]] * 2, acc=both, name="att_mid")
    t_sums = text_attention(after(txt, both[0]), kv, n_patch)
    t_got = lax.all_to_all(t_sums, "patch", 0, 0)
    num, den, part_c = attention(
        after(pos, t_sums),
        [q, q_c],
        [kvz_m, kvz_p, kvz_2],
        [[0, 1, 2]] * 2,
        acc=both,
        packed=(1,),
        name="att_last",
    )
    got_c = send_patch(part_c, dc=1)
    attn = quotient(text_len, q, txt, num, den, after(got_c, proj_z))
    from_z = send_head(attn, dz=1)
    t_proj = text_quotient(text_len, after(t_got, attn), t_q, txt, txt_proj, n_head)
    outs = project(pos, attn, from_z, img_proj, proj_z)
    img_sum = exchange(outs)
    column = me_h * width
    img_gate = lax.dynamic_slice_in_dim(img_mod[2], column, width)
    img_out = (image.astype(F32) + img_gate * img_sum).astype(BF)
    t_sum = lax.all_to_all(t_proj, "head", 0, 0).astype(F32).sum(axis=0)
    txt_gate = lax.dynamic_slice_in_dim(txt_mod[2], column, width)
    t_out = (t_own.astype(F32) + txt_gate * t_sum).astype(BF)
    txt_out = lax.all_to_all(
        jnp.broadcast_to(t_out[None], (n_patch,) + t_out.shape), "patch", 0, 0
    ).reshape(txt_total, width)
    return (img_out, txt_out)


def solution(mesh):
    in_specs = (
        P("patch", "head"),
        P(None, "head"),
        P(),
        P(),
        P(),
        P(None, None, "head"),
        P(None, None, "head"),
        P("head", None),
        P("head", None),
        P(),
        P(),
        P(None, "patch", "head"),
    )
    out_specs = (P("patch", "head"), P(None, "head"))
    return jax.shard_map(shards, mesh=mesh, in_specs=in_specs, out_specs=out_specs, check_vma=False)
```

```python
import functools
import math

import jax
import jax.numpy as jnp
from jax import lax
from jax.experimental import pallas as pl
from jax.experimental.pallas import tpu as pltpu
from jax.sharding import PartitionSpec as P

EPS_NORM = 1e-06
BF = jnp.bfloat16
F32 = jnp.float32
VMEM = 56 * 2**20
NX, NY = 4, 4
TINY = pl.CostEstimate(flops=1, bytes_accessed=1, transcendentals=0)


def cost(us):
    return pl.CostEstimate(flops=int(us * 1.15e9), bytes_accessed=1, transcendentals=0)


def patch_perm(dz, dx, dc):
    return [
        ((z * NX + x) * 2 + c, ((z ^ dz) * NX + (x + dx) % NX) * 2 + (c ^ dc))
        for z in range(2)
        for x in range(NX)
        for c in range(2)
    ]


def head_perm(dz, dy):
    return [(z * NY + y, (z ^ dz) * NY + (y + dy) % NY) for z in range(2) for y in range(NY)]


def send_patch(x, dz=0, dx=0, dc=0):
    return lax.ppermute(x, "patch", patch_perm(dz, dx, dc))


def send_head(x, dz=0, dy=0):
    return lax.ppermute(x, "head", head_perm(dz, dy))


def in_hbm(x):
    return pltpu.with_memory_space_constraint(x, pltpu.HBM)


def after(x, *deps):
    return lax.optimization_barrier((x,) + deps)[0]


def lane_sum(parts, hd):
    acc = None
    for p in parts:
        for c in range(0, p.shape[1], hd):
            piece = p[:, c : c + hd]
            acc = piece if acc is None else acc + piece
    return jnp.sum(acc, axis=-1, keepdims=True)


def moments(vals, hd):
    mean = lane_sum(vals, hd) * (1.0 / sum(v.shape[1] for v in vals))
    vals = [v - mean for v in vals]
    return mean, vals, lane_sum([v * v for v in vals], hd)


def rms_heads(mixed, gain):
    hd = gain.shape[1]
    heads = []
    for c in range(0, mixed.shape[1], hd):
        v = mixed[:, c : c + hd]
        rms = lax.rsqrt(jnp.mean(v * v, axis=-1, keepdims=True) + EPS_NORM)
        heads.append((v * rms * gain).astype(BF))
    return jnp.concatenate(heads, axis=1)


def query_scale(hd):
    return hd ** (-0.5) * math.log2(math.e)


def weight_copies(idx_ref, w_ref, w_buf, sem, first):
    width = w_ref.shape[2]
    return [
        pltpu.make_async_copy(
            w_ref.at[p, pl.ds(pl.multiple_of(idx_ref[first + n] * width, width), width)],
            w_buf.at[pl.ds(n * width, width), pl.ds(p * width, width)],
            sem.at[p, n],
        )
        for n in range(sem.shape[1])
        for p in range(3)
    ]


def early_kernel(idx_ref, *refs, blocks, rows):
    x_refs = refs[:blocks]
    w_ref, mod_ref, acc_ref, stat_ref, x_buf, w_buf, mod_buf, x_sem, w_sem = refs[blocks:]
    width = x_buf.shape[2]
    hd = stat_ref.shape[2]
    x_copies = [
        pltpu.make_async_copy(x_refs[n].at[pl.ds(0, rows)], x_buf.at[n], x_sem.at[n]) for n in range(blocks)
    ]
    w_copies = weight_copies(idx_ref, w_ref, w_buf, w_sem, 0)
    for copy in x_copies + w_copies:
        copy.start()
    for n in range(blocks):
        cols = slice(n * width, (n + 1) * width)
        m = mod_ref[idx_ref[n]]
        scale, shift = 1.0 + m[1:2], m[0:1]
        high, low = [v.astype(BF) for v in (scale, shift)]
        pieces = [high, (scale - high.astype(F32)).astype(BF), low, (shift - low.astype(F32)).astype(BF)]
        tail = mod_buf.shape[0] - rows - len(pieces)
        mod_buf[rows:, cols] = jnp.concatenate(pieces + [jnp.zeros((tail, width), BF)], axis=0)
    for copy in x_copies:
        copy.wait()
    for o in range(0, rows, 16):
        mean, vals, square = moments([x_buf[n, o : o + 16].astype(F32) for n in range(blocks)], hd)
        inverse = lax.rsqrt(square * (1.0 / (blocks * width)) + EPS_NORM)
        stat_ref[0, o : o + 16] = jnp.broadcast_to(mean, (16, hd))
        stat_ref[1, o : o + 16] = jnp.broadcast_to(square, (16, hd))
        for n, v in enumerate(vals):
            out = v * inverse * (1.0 + mod_ref[idx_ref[n]][1:2])
            mod_buf[o : o + 16, n * width : (n + 1) * width] = out.astype(BF)
    for copy in w_copies:
        copy.wait()
    acc_ref[...] = jnp.dot(mod_buf[...], w_buf[...], preferred_element_type=F32)


def late_kernel(idx_ref, *refs, first, tile, scale):
    lone = len(refs) - 15
    x_refs = list(refs[:lone]) + [refs[lone].at[0], refs[lone].at[1]]
    w_ref, acc_hbm, stat_ref, mod_ref, gain_ref, q_ref, kv_ref = refs[lone + 1 : lone + 8]
    x_buf, w_buf, acc_ref, mod_buf, x_sem, w_sem, acc_sem = refs[lone + 8 :]
    blocks, rows, width = x_buf.shape
    hd = gain_ref.shape[1]
    tiles = rows // tile
    n_first, n_last = first * width, blocks * width
    x_copies = [
        [
            pltpu.make_async_copy(
                x_refs[n].at[pl.ds(t * tile, tile)], x_buf.at[n, pl.ds(t * tile, tile)], x_sem.at[t, n]
            )
            for n in range(blocks)
        ]
        for t in range(tiles)
    ]
    w_copies = weight_copies(idx_ref, w_ref, w_buf, w_sem, first)
    acc_copy = pltpu.make_async_copy(acc_hbm, acc_ref, acc_sem)
    for copy in x_copies[0] + w_copies + [acc_copy] + sum(x_copies[1:], []):
        copy.start()
    factors = {}

    def normalise(t):
        for copy in x_copies[t]:
            copy.wait()
        ratios, shifts = [], []
        for o in range(t * tile, (t + 1) * tile, 16):
            mean, vals, square = moments([x_buf[n, o : o + 16].astype(F32) for n in range(blocks)], hd)
            mean0 = stat_ref[0, o : o + 16, 0:1]
            square0 = stat_ref[1, o : o + 16, 0:1]
            gap = mean0 - mean
            total = square + square0 + gap * gap * (n_first * n_last / (n_first + n_last))
            inverse = lax.rsqrt(total * (1.0 / (n_first + n_last)) + EPS_NORM)
            center = mean + gap * (n_first / (n_first + n_last))
            ratios.append(inverse * jnp.sqrt(square0 * (1.0 / n_first) + EPS_NORM))
            shifts.append((mean0 - center) * inverse)
            for n, v in enumerate(vals):
                m = mod_ref[idx_ref[first + n]]
                out = (v + (mean - center)) * inverse * (1.0 + m[1:2]) + m[0:1]
                mod_buf[o : o + 16, n * width : (n + 1) * width] = out.astype(BF)
        factors[t] = (jnp.concatenate(ratios, axis=0), jnp.concatenate(shifts, axis=0))

    normalise(0)
    for copy in w_copies + [acc_copy]:
        copy.wait()
    scales = acc_ref[rows : rows + 1] + acc_ref[rows + 1 : rows + 2]
    offset = acc_ref[rows + 2 : rows + 3] + acc_ref[rows + 3 : rows + 4]
    for t in range(tiles):
        part = slice(t * tile, (t + 1) * tile)
        mixed = jnp.dot(mod_buf[part], w_buf[...], preferred_element_type=F32)
        if t + 1 < tiles:
            normalise(t + 1)
        ratio, shift = factors[t]
        mixed = mixed + acc_ref[part] * ratio + shift * scales + offset
        q_ref[part] = rms_heads(mixed[:, :width], gain_ref[0:1] * scale)
        kv_ref[0, part] = rms_heads(mixed[:, width : 2 * width], gain_ref[1:2])
        kv_ref[1, part] = mixed[:, 2 * width :].astype(BF)


def early_qkv(idx, x_list, w, mod, rows):
    width = x_list[0].shape[1]
    n = len(x_list)
    hd = 128
    hbm = pl.BlockSpec(memory_space=pltpu.HBM)
    vmem = pl.BlockSpec(memory_space=pltpu.VMEM)
    return pl.pallas_call(
        functools.partial(early_kernel, blocks=n, rows=rows),
        in_specs=[pl.BlockSpec(memory_space=pltpu.SMEM)] + [hbm] * (n + 1) + [vmem],
        out_specs=[vmem] * 2,
        out_shape=[
            jax.ShapeDtypeStruct((rows + 16, 3 * width), F32),
            jax.ShapeDtypeStruct((2, rows, hd), F32),
        ],
        scratch_shapes=[
            pltpu.VMEM((n, rows, width), BF),
            pltpu.VMEM((n * width, 3 * width), BF),
            pltpu.VMEM((rows + 16, n * width), BF),
            pltpu.SemaphoreType.DMA((n,)),
            pltpu.SemaphoreType.DMA((3, n)),
        ],
        compiler_params=pltpu.CompilerParams(vmem_limit_bytes=VMEM),
        cost_estimate=TINY,
        name="early_qkv",
    )(idx, *x_list, w, mod)


def late_qkv(idx, x_list, w, acc, stat, mod, gain):
    rows, width = stat.shape[1], x_list[0].shape[1]
    n = len(x_list) + 1
    first = mod.shape[0] - n
    tile = rows // 2
    hbm = pl.BlockSpec(memory_space=pltpu.HBM)
    vmem = pl.BlockSpec(memory_space=pltpu.VMEM)
    return pl.pallas_call(
        functools.partial(
            late_kernel, first=first, tile=tile, scale=query_scale(gain.shape[1])
        ),
        in_specs=[pl.BlockSpec(memory_space=pltpu.SMEM)] + [hbm] * (n + 1) + [vmem] * 3,
        out_specs=[vmem] * 2,
        out_shape=[
            jax.ShapeDtypeStruct((rows, width), BF),
            jax.ShapeDtypeStruct((2, rows, width), BF),
        ],
        scratch_shapes=[
            pltpu.VMEM((n, rows, width), BF),
            pltpu.VMEM((n * width, 3 * width), BF),
            pltpu.VMEM(acc.shape, F32),
            pltpu.VMEM((rows, n * width), BF),
            pltpu.SemaphoreType.DMA((2, n)),
            pltpu.SemaphoreType.DMA((3, n)),
            pltpu.SemaphoreType.DMA,
        ],
        compiler_params=pltpu.CompilerParams(vmem_limit_bytes=VMEM),
        cost_estimate=TINY,
        name="late_qkv",
    )(idx, *x_list, w, acc, stat, mod, gain)


def text_qkv_kernel(idx_ref, *refs, blocks, scale):
    x_refs = list(refs[: blocks - 2]) + [refs[blocks - 2].at[0], refs[blocks - 2].at[1]]
    w_ref, mod_ref, gain_ref, out_ref, mod_buf = refs[blocks - 1 :]
    width = x_refs[0].shape[1]
    vals = [r[...].astype(F32) for r in x_refs]
    _, vals, square = moments(vals, gain_ref.shape[1])
    inverse = lax.rsqrt(square * (1.0 / (blocks * width)) + EPS_NORM)
    for n, v in enumerate(vals):
        m = mod_ref[idx_ref[n]]
        out = (v * inverse * (1.0 + m[1:2]) + m[0:1]).astype(BF)
        mod_buf[:, pl.ds(pl.multiple_of(idx_ref[n] * width, 128), width)] = out
    mixed = [jnp.dot(mod_buf[...], w_ref[p], preferred_element_type=F32) for p in range(3)]
    out_ref[:, :width] = rms_heads(mixed[0], gain_ref[0:1] * scale)
    out_ref[:, width : 2 * width] = rms_heads(mixed[1], gain_ref[1:2])
    out_ref[:, 2 * width :] = mixed[2].astype(BF)


def text_qkv(idx, x_list, w, mod, gain, rows):
    total, width = x_list[0].shape
    n = len(x_list) + 1
    last = total // rows - 1
    vmem = pl.BlockSpec(memory_space=pltpu.VMEM)
    return pl.pallas_call(
        functools.partial(text_qkv_kernel, blocks=n, scale=query_scale(gain.shape[1])),
        grid=(1,),
        in_specs=[pl.BlockSpec(memory_space=pltpu.SMEM)]
        + [pl.BlockSpec((rows, width), lambda i: (last, 0))] * (n - 2)
        + [pl.BlockSpec((2, rows, width), lambda i: (0, last, 0))]
        + [vmem] * 3,
        out_specs=vmem,
        out_shape=jax.ShapeDtypeStruct((rows, 3 * width), BF),
        scratch_shapes=[pltpu.VMEM((rows, n * width), BF)],
        compiler_params=pltpu.CompilerParams(vmem_limit_bytes=24 * 2**20),
        cost_estimate=cost(2),
        name="text_qkv",
    )(idx, *[in_hbm(x) for x in x_list], w, mod, gain)


def one(q, k, v, valid=None):
    s = lax.dot_general(q, k, (((1,), (1,)), ((), ())), preferred_element_type=F32)
    e = jnp.exp2(s)
    if valid is not None:
        e = jnp.where(lax.broadcasted_iota(jnp.int32, e.shape, 1) < valid, e, 0.0)
    hd = v.shape[1]
    wide = jnp.concatenate([v, jnp.ones_like(v)], axis=1)
    both = jnp.dot(e.astype(BF), wide, preferred_element_type=F32)
    return both[:, :hd], both[:, hd:]


def att_kernel(pos_ref, *refs, plan, n_q, n_kv, text, acc, packed):
    refs = list(refs)
    length = refs.pop(0) if text else None
    qs = [refs.pop(0) for _ in range(n_q)]
    kvs = [refs.pop(0) for _ in range(n_kv)]
    txt = [refs.pop(0) for _ in range(2)] if text else None
    accs = [refs.pop(0) for _ in range(2 * n_q)] if acc else None
    for i in range(n_q):
        num = accs[2 * i][...] if acc else None
        den = accs[2 * i + 1][...] if acc else None
        q = qs[i][...]
        parts = [(kvs[j].at[0], kvs[j].at[1], None) for j in plan[i]]
        if text and i == 0:
            parts.append((txt[0], txt[1], length[0]))
        for k_ref, v_ref, valid in parts:
            n, d = one(q, k_ref[...], v_ref[...], valid)
            num = n if num is None else num + n
            den = d if den is None else den + d
        if i in packed:
            out = refs.pop(0)
            out[0] = num.astype(BF)
            out[1] = den.astype(BF)
        else:
            refs.pop(0)[...] = num
            refs.pop(0)[...] = den


def attention(pos, qs, kvs, plan, text=None, acc=None, packed=(), name="att"):
    rows, width = qs[0].shape
    hd = 128
    heads = width // hd
    n_q = len(qs)
    args, specs = [], []
    if text is not None:
        args.append(text[0])
        specs.append(pl.BlockSpec(memory_space=pltpu.SMEM))
    q_spec = pl.BlockSpec((rows, hd), lambda h, p: (0, h))
    out_spec = pl.BlockSpec((rows, hd), lambda h, p: (0, h))
    for q in qs:
        args.append(q)
        specs.append(q_spec)
    keys = 0
    for kv in kvs:
        keys = kv.shape[1]
        specs.append(pl.BlockSpec((2, keys, hd), lambda h, p: (0, 0, h)))
        args.append(kv)
    if text is not None:
        tk = text[1]
        args += [tk, tk]
        specs.append(pl.BlockSpec((tk.shape[0], hd), lambda h, p: (0, heads + h)))
        specs.append(pl.BlockSpec((tk.shape[0], hd), lambda h, p: (0, 2 * heads + h)))
    if acc is not None:
        args += list(acc)
        specs += [q_spec] * len(acc)
    outs, out_specs = [], []
    for i in range(n_q):
        if i in packed:
            outs.append(jax.ShapeDtypeStruct((2, rows, width), BF))
            out_specs.append(pl.BlockSpec((2, rows, hd), lambda h, p: (0, 0, h)))
        else:
            outs += [jax.ShapeDtypeStruct((rows, width), F32)] * 2
            out_specs += [out_spec] * 2
    blocks = sum(len(p) for p in plan)
    return pl.pallas_call(
        functools.partial(
            att_kernel, plan=plan, n_q=n_q, n_kv=len(kvs), text=text is not None, acc=acc is not None, packed=packed
        ),
        grid_spec=pltpu.PrefetchScalarGridSpec(
            num_scalar_prefetch=1, grid=(heads,), in_specs=specs, out_specs=out_specs
        ),
        out_shape=outs,
        compiler_params=pltpu.CompilerParams(vmem_limit_bytes=VMEM),
        cost_estimate=pl.CostEstimate(
            flops=14 * rows * keys * width * blocks, bytes_accessed=1, transcendentals=0
        ),
        name=name,
    )(pos, *args)


def text_att_kernel(q_ref, kv_ref, out_ref):
    n_patch, _, rows, width = out_ref.shape
    hd = 128
    for h in range(width // hd):
        cols = slice(h * hd, (h + 1) * hd)
        num, den = one(q_ref[:, cols], kv_ref[0, :, cols], kv_ref[1, :, cols])
        out_ref[:, 0, :, cols] = num.astype(BF).reshape(n_patch, rows, hd)
        out_ref[:, 1, :, cols] = den.astype(BF).reshape(n_patch, rows, hd)


def text_attention(txt, kv, n_patch):
    rows = txt.shape[0]
    width = kv.shape[2]
    return pl.pallas_call(
        text_att_kernel,
        grid=(1,),
        in_specs=[pl.BlockSpec((rows, width), lambda i: (0, 0)), pl.BlockSpec(kv.shape, lambda i: (0, 0, 0))],
        out_specs=pl.BlockSpec((n_patch, 2, rows // n_patch, width), lambda i: (0, 0, 0, 0)),
        out_shape=jax.ShapeDtypeStruct((n_patch, 2, rows // n_patch, width), BF),
        compiler_params=pltpu.CompilerParams(vmem_limit_bytes=VMEM),
        cost_estimate=cost(3),
        name="text_attention",
    )(txt, kv)


def text_keys(q_ref, txt_ref, len_ref, h):
    hd = 128
    width = q_ref.shape[1]
    at = h * hd
    k = txt_ref[:, width + at : width + at + hd]
    v = txt_ref[:, 2 * width + at : 2 * width + at + hd]
    return one(q_ref[:, at : at + hd], k, v, len_ref[0])


def image_quotient(len_ref, q_ref, txt_ref, num_ref, den_ref, got_ref, attn_ref):
    hd = 128
    for h in range(num_ref.shape[1] // hd):
        cols = slice(h * hd, (h + 1) * hd)
        n, d = text_keys(q_ref, txt_ref, len_ref, h)
        num = n + num_ref[:, cols] + got_ref[0, :, cols].astype(F32)
        den = d + den_ref[:, cols] + got_ref[1, :, cols].astype(F32)
        attn_ref[:, cols] = (num / den).astype(BF)


def quotient(text_len, q, txt, num, den, got):
    vmem = pl.BlockSpec(memory_space=pltpu.VMEM)
    return pl.pallas_call(
        image_quotient,
        in_specs=[pl.BlockSpec(memory_space=pltpu.SMEM)] + [vmem] * 5,
        out_specs=vmem,
        out_shape=jax.ShapeDtypeStruct(q.shape, BF),
        compiler_params=pltpu.CompilerParams(vmem_limit_bytes=VMEM),
        cost_estimate=cost(4),
        name="quotient",
    )(text_len, q, txt, num, den, got)


def text_quotient_kernel(len_ref, sum_ref, q_ref, txt_ref, proj_ref, out_ref):
    rows, width = q_ref.shape
    hd = 128
    parts = []
    for h in range(width // hd):
        cols = slice(h * hd, (h + 1) * hd)
        n, d = text_keys(q_ref, txt_ref, len_ref, h)
        num = n + jnp.sum(sum_ref[:, 0, :, cols].astype(F32), axis=0)
        den = d + jnp.sum(sum_ref[:, 1, :, cols].astype(F32), axis=0)
        parts.append((num / den).astype(BF))
    attn = jnp.concatenate(parts, axis=1)
    part = jnp.dot(attn, proj_ref[...], preferred_element_type=F32).astype(BF)
    for j in range(out_ref.shape[0]):
        out_ref[j] = part[:, j * width : (j + 1) * width]


def text_quotient(text_len, sums, q, txt, proj, n_head):
    vmem = pl.BlockSpec(memory_space=pltpu.VMEM)
    return pl.pallas_call(
        text_quotient_kernel,
        in_specs=[pl.BlockSpec(memory_space=pltpu.SMEM)] + [vmem] * 4,
        out_specs=vmem,
        out_shape=jax.ShapeDtypeStruct((n_head,) + q.shape, BF),
        compiler_params=pltpu.CompilerParams(vmem_limit_bytes=VMEM),
        cost_estimate=cost(4),
        name="text_quotient",
    )(text_len, sums, q, txt, proj)


def proj_kernel(pos_ref, mine_ref, got_ref, w_ref, wz_ref, wc_ref, *refs):
    outs = refs[:NY]
    w_buf, sem = refs[NY:]
    width = mine_ref.shape[1]
    zh, y, core = pos_ref[0], pos_ref[1], pos_ref[2]
    half = width // 2
    order = (2, 1, 3, 0)

    def copies(d):
        block = lax.rem(y + d, NY)
        sources = (
            (w_ref, zh * NY + block, 0, width),
            (wz_ref, block, width + core * half, half),
            (wc_ref, block, width + (1 - core) * half, half),
        )
        return [
            pltpu.make_async_copy(
                ref.at[:, pl.ds(pl.multiple_of(at * width, 128), width)],
                w_buf.at[d, pl.ds(row if i == 0 else pl.multiple_of(row, half), size)],
                sem.at[d, i],
            )
            for i, (ref, at, row, size) in enumerate(sources)
        ]

    for d in order:
        for copy in copies(d):
            copy.start()
    both = jnp.concatenate([mine_ref[...], got_ref[...]], axis=1)
    for d in order:
        for copy in copies(d):
            copy.wait()
        outs[d][...] = jnp.dot(both, w_buf[d], preferred_element_type=F32).astype(BF)


def project(pos, mine, got, w, wz, wc):
    width = mine.shape[1]
    spec = pl.BlockSpec(memory_space=pltpu.VMEM)
    hbm = pl.BlockSpec(memory_space=pltpu.HBM)
    return pl.pallas_call(
        proj_kernel,
        in_specs=[pl.BlockSpec(memory_space=pltpu.SMEM)] + [spec] * 2 + [hbm] * 3,
        out_specs=[spec] * NY,
        out_shape=[jax.ShapeDtypeStruct(mine.shape, BF)] * NY,
        scratch_shapes=[
            pltpu.VMEM((NY, 2 * width, width), BF),
            pltpu.SemaphoreType.DMA((NY, 3)),
        ],
        compiler_params=pltpu.CompilerParams(vmem_limit_bytes=VMEM),
        cost_estimate=cost(6),
        name="project",
    )(pos, mine, got, w, wz, wc)


def exchange(parts):
    total = parts[0].astype(F32)
    for d in range(1, NY):
        total = total + send_head(parts[d], dy=d).astype(F32)
    return total


def shards(
    image,
    text,
    text_len,
    img_mod,
    txt_mod,
    img_qkv,
    txt_qkv,
    img_proj,
    txt_proj,
    img_gain,
    txt_gain,
    stale_kv,
):
    n_head = lax.axis_size("head")
    n_patch = lax.axis_size("patch")
    me_h = lax.axis_index("head")
    me_p = lax.axis_index("patch")
    zh, y = me_h // NY, me_h % NY
    group, width = image.shape
    txt_total = text.shape[0]
    t_rows = txt_total // n_patch

    pos = jnp.stack([zh, y, me_p % 2]).astype(jnp.int32)

    t_own = lax.dynamic_slice_in_dim(text, me_p * t_rows, t_rows, 0)
    rows = jnp.concatenate([image, t_own], axis=0)
    i_z = send_head(rows, dz=1)
    i_m = send_head(rows, dy=1)
    i_p = send_head(rows, dy=-1)
    kv_m = send_patch(stale_kv, dx=1)
    core = me_p % 2
    part_z = lax.dynamic_slice(
        img_proj, (core * (width // 2), (1 - zh) * NY * width), (width // 2, NY * width)
    )
    near = after(i_z, i_m, i_p, part_z)
    ahead = send_head(jnp.stack([i_m, near]), dy=1)
    iz_p = send_head(near, dy=-1)
    mod_i = img_mod.reshape(3, n_head, width).transpose(1, 0, 2)
    mod_t = txt_mod.reshape(3, n_head, width).transpose(1, 0, 2)
    ring = (y + jnp.array([0, 0, NY - 1, 1, 1, 2, 2, NY - 1])) % NY
    side = (zh + jnp.array([0, 1, 0, 0, 1, 1, 0, 1])) % 2
    idx = (side * NY + ring).astype(jnp.int32)
    w_i = img_qkv.transpose(1, 0, 2)
    iz_2 = send_head(iz_p, dy=-1)
    acc, stat = early_qkv(after(idx, kv_m, iz_p), [rows, near, i_m, i_p], w_i, mod_i, group)
    later = after(stale_kv, iz_p)
    kv_z = send_patch(later, dz=1)
    kv_p = send_patch(later, dx=-1)
    kv_2 = send_patch(kv_m, dx=1)
    kvz_m = send_patch(kv_z, dx=1)
    kvz_p = send_patch(kv_z, dx=-1)
    kvz_2 = send_patch(kv_2, dz=1)
    proj_z = send_head(after(part_z, kv_z), dz=1)
    proj_c = send_patch(proj_z, dc=1)
    q, kv = late_qkv(idx, [iz_p, iz_2, ahead], w_i, acc, stat, mod_i, img_gain)
    x_list = [rows, near, i_m, i_p, iz_p, iz_2, ahead]
    q_c = send_patch(q, dc=1)
    t_pack = text_qkv(after(idx, q), x_list, txt_qkv.transpose(1, 0, 2), mod_t, txt_gain, t_rows)
    t_q = t_pack[:, :width]
    txt = lax.all_to_all(
        jnp.broadcast_to(t_pack[None], (n_patch,) + t_pack.shape), "patch", 0, 0
    ).reshape(txt_total, 3 * width)

    both = attention(
        after(pos, t_pack),
        [q, q_c],
        [kv, stale_kv, kv_m, kv_p, kv_2, kv_z],
        [[0, 2, 3, 4, 5], [1, 2, 3, 4, 5]],
        name="att_near",
    )
    t_sums = text_attention(after(txt, both[0]), kv, n_patch)
    t_got = lax.all_to_all(t_sums, "patch", 0, 0)
    num, den, part_c = attention(
        after(pos, t_sums),
        [q, q_c],
        [kvz_m, kvz_p, kvz_2],
        [[0, 1, 2]] * 2,
        acc=both,
        packed=(1,),
        name="att_last",
    )
    got_c = send_patch(part_c, dc=1)
    attn = quotient(text_len, q, txt, num, den, after(got_c, proj_c))
    from_z = send_head(attn, dz=1)
    t_proj = text_quotient(text_len, after(t_got, attn), t_q, txt, txt_proj, n_head)
    img_sum = exchange(project(pos, attn, from_z, img_proj, proj_z, proj_c))
    column = me_h * width
    img_gate = lax.dynamic_slice_in_dim(img_mod[2], column, width)
    img_out = (image.astype(F32) + img_gate * img_sum).astype(BF)
    t_sum = lax.all_to_all(t_proj, "head", 0, 0).astype(F32).sum(axis=0)
    txt_gate = lax.dynamic_slice_in_dim(txt_mod[2], column, width)
    t_out = (t_own.astype(F32) + txt_gate * t_sum).astype(BF)
    txt_out = lax.all_to_all(
        jnp.broadcast_to(t_out[None], (n_patch,) + t_out.shape), "patch", 0, 0
    ).reshape(txt_total, width)
    return (img_out, txt_out)


def solution(mesh):
    in_specs = (
        P("patch", "head"),
        P(None, "head"),
        P(),
        P(),
        P(),
        P(None, None, "head"),
        P(None, None, "head"),
        P("head", None),
        P("head", None),
        P(),
        P(),
        P(None, "patch", "head"),
    )
    out_specs = (P("patch", "head"), P(None, "head"))
    return jax.shard_map(shards, mesh=mesh, in_specs=in_specs, out_specs=out_specs, check_vma=False)
```

```python
import functools
import math

import jax
import jax.numpy as jnp
from jax import lax
from jax.experimental import pallas as pl
from jax.experimental.pallas import tpu as pltpu
from jax.sharding import PartitionSpec as P

EPS_NORM = 1e-06
BF = jnp.bfloat16
F32 = jnp.float32
VMEM = 56 * 2**20
NX, NY = 4, 4
TINY = pl.CostEstimate(flops=1, bytes_accessed=1, transcendentals=0)


def cost(us):
    return pl.CostEstimate(flops=int(us * 1.15e9), bytes_accessed=1, transcendentals=0)


def patch_perm(dz, dx, dc):
    return [
        ((z * NX + x) * 2 + c, ((z ^ dz) * NX + (x + dx) % NX) * 2 + (c ^ dc))
        for z in range(2)
        for x in range(NX)
        for c in range(2)
    ]


def head_perm(dz, dy):
    return [(z * NY + y, (z ^ dz) * NY + (y + dy) % NY) for z in range(2) for y in range(NY)]


def send_patch(x, dz=0, dx=0, dc=0):
    return lax.ppermute(x, "patch", patch_perm(dz, dx, dc))


def send_head(x, dz=0, dy=0):
    return lax.ppermute(x, "head", head_perm(dz, dy))


def in_hbm(x):
    return pltpu.with_memory_space_constraint(x, pltpu.HBM)


def after(x, *deps):
    return lax.optimization_barrier((x,) + deps)[0]


def lane_sum(parts, hd):
    acc = None
    for p in parts:
        for c in range(0, p.shape[1], hd):
            piece = p[:, c : c + hd]
            acc = piece if acc is None else acc + piece
    return jnp.sum(acc, axis=-1, keepdims=True)


def moments(vals, hd):
    mean = lane_sum(vals, hd) * (1.0 / sum(v.shape[1] for v in vals))
    vals = [v - mean for v in vals]
    return mean, vals, lane_sum([v * v for v in vals], hd)


def rms_heads(mixed, gain):
    hd = gain.shape[1]
    heads = []
    for c in range(0, mixed.shape[1], hd):
        v = mixed[:, c : c + hd]
        rms = lax.rsqrt(jnp.mean(v * v, axis=-1, keepdims=True) + EPS_NORM)
        heads.append((v * rms * gain).astype(BF))
    return jnp.concatenate(heads, axis=1)


def query_scale(hd):
    return hd ** (-0.5) * math.log2(math.e)


def weight_copies(idx_ref, w_ref, w_buf, sem, first):
    width = w_ref.shape[2]
    return [
        pltpu.make_async_copy(
            w_ref.at[p, pl.ds(pl.multiple_of(idx_ref[first + n] * width, width), width)],
            w_buf.at[pl.ds(n * width, width), pl.ds(p * width, width)],
            sem.at[p, n],
        )
        for n in range(sem.shape[1])
        for p in range(3)
    ]


def early_kernel(idx_ref, *refs, blocks, rows):
    x_refs = refs[:blocks]
    w_ref, mod_ref, acc_ref, stat_ref, x_buf, w_buf, mod_buf, x_sem, w_sem = refs[blocks:]
    width = x_buf.shape[2]
    hd = stat_ref.shape[2]
    x_copies = [
        pltpu.make_async_copy(x_refs[n].at[pl.ds(0, rows)], x_buf.at[n], x_sem.at[n]) for n in range(blocks)
    ]
    w_copies = weight_copies(idx_ref, w_ref, w_buf, w_sem, 0)
    for copy in x_copies + w_copies:
        copy.start()
    for n in range(blocks):
        cols = slice(n * width, (n + 1) * width)
        m = mod_ref[idx_ref[n]]
        scale, shift = 1.0 + m[1:2], m[0:1]
        high, low = [v.astype(BF) for v in (scale, shift)]
        pieces = [high, (scale - high.astype(F32)).astype(BF), low, (shift - low.astype(F32)).astype(BF)]
        tail = mod_buf.shape[0] - rows - len(pieces)
        mod_buf[rows:, cols] = jnp.concatenate(pieces + [jnp.zeros((tail, width), BF)], axis=0)
    for copy in x_copies:
        copy.wait()
    for o in range(0, rows, 16):
        mean, vals, square = moments([x_buf[n, o : o + 16].astype(F32) for n in range(blocks)], hd)
        inverse = lax.rsqrt(square * (1.0 / (blocks * width)) + EPS_NORM)
        stat_ref[0, o : o + 16] = jnp.broadcast_to(mean, (16, hd))
        stat_ref[1, o : o + 16] = jnp.broadcast_to(square, (16, hd))
        for n, v in enumerate(vals):
            out = v * inverse * (1.0 + mod_ref[idx_ref[n]][1:2])
            mod_buf[o : o + 16, n * width : (n + 1) * width] = out.astype(BF)
    for copy in w_copies:
        copy.wait()
    acc_ref[...] = jnp.dot(mod_buf[...], w_buf[...], preferred_element_type=F32)


def late_kernel(idx_ref, *refs, first, tile, scale):
    lone = len(refs) - 15
    x_refs = list(refs[:lone]) + [refs[lone].at[0], refs[lone].at[1]]
    w_ref, acc_hbm, stat_ref, mod_ref, gain_ref, q_ref, kv_ref = refs[lone + 1 : lone + 8]
    x_buf, w_buf, acc_ref, mod_buf, x_sem, w_sem, acc_sem = refs[lone + 8 :]
    blocks, rows, width = x_buf.shape
    hd = gain_ref.shape[1]
    tiles = rows // tile
    n_first, n_last = first * width, blocks * width
    x_copies = [
        [
            pltpu.make_async_copy(
                x_refs[n].at[pl.ds(t * tile, tile)], x_buf.at[n, pl.ds(t * tile, tile)], x_sem.at[t, n]
            )
            for n in range(blocks)
        ]
        for t in range(tiles)
    ]
    w_copies = weight_copies(idx_ref, w_ref, w_buf, w_sem, first)
    acc_copy = pltpu.make_async_copy(acc_hbm, acc_ref, acc_sem)
    for copy in x_copies[0] + w_copies + [acc_copy] + sum(x_copies[1:], []):
        copy.start()
    factors = {}

    def normalise(t):
        for copy in x_copies[t]:
            copy.wait()
        ratios, shifts = [], []
        for o in range(t * tile, (t + 1) * tile, 16):
            mean, vals, square = moments([x_buf[n, o : o + 16].astype(F32) for n in range(blocks)], hd)
            mean0 = stat_ref[0, o : o + 16, 0:1]
            square0 = stat_ref[1, o : o + 16, 0:1]
            gap = mean0 - mean
            total = square + square0 + gap * gap * (n_first * n_last / (n_first + n_last))
            inverse = lax.rsqrt(total * (1.0 / (n_first + n_last)) + EPS_NORM)
            center = mean + gap * (n_first / (n_first + n_last))
            ratios.append(inverse * jnp.sqrt(square0 * (1.0 / n_first) + EPS_NORM))
            shifts.append((mean0 - center) * inverse)
            for n, v in enumerate(vals):
                m = mod_ref[idx_ref[first + n]]
                out = (v + (mean - center)) * inverse * (1.0 + m[1:2]) + m[0:1]
                mod_buf[o : o + 16, n * width : (n + 1) * width] = out.astype(BF)
        factors[t] = (jnp.concatenate(ratios, axis=0), jnp.concatenate(shifts, axis=0))

    normalise(0)
    for copy in w_copies + [acc_copy]:
        copy.wait()
    scales = acc_ref[rows : rows + 1] + acc_ref[rows + 1 : rows + 2]
    offset = acc_ref[rows + 2 : rows + 3] + acc_ref[rows + 3 : rows + 4]
    for t in range(tiles):
        part = slice(t * tile, (t + 1) * tile)
        mixed = jnp.dot(mod_buf[part], w_buf[...], preferred_element_type=F32)
        if t + 1 < tiles:
            normalise(t + 1)
        ratio, shift = factors[t]
        mixed = mixed + acc_ref[part] * ratio + shift * scales + offset
        q_ref[part] = rms_heads(mixed[:, :width], gain_ref[0:1] * scale)
        kv_ref[0, part] = rms_heads(mixed[:, width : 2 * width], gain_ref[1:2])
        kv_ref[1, part] = mixed[:, 2 * width :].astype(BF)


def early_qkv(idx, x_list, w, mod, rows):
    width = x_list[0].shape[1]
    n = len(x_list)
    hd = 128
    hbm = pl.BlockSpec(memory_space=pltpu.HBM)
    vmem = pl.BlockSpec(memory_space=pltpu.VMEM)
    return pl.pallas_call(
        functools.partial(early_kernel, blocks=n, rows=rows),
        in_specs=[pl.BlockSpec(memory_space=pltpu.SMEM)] + [hbm] * (n + 1) + [vmem],
        out_specs=[vmem] * 2,
        out_shape=[
            jax.ShapeDtypeStruct((rows + 16, 3 * width), F32),
            jax.ShapeDtypeStruct((2, rows, hd), F32),
        ],
        scratch_shapes=[
            pltpu.VMEM((n, rows, width), BF),
            pltpu.VMEM((n * width, 3 * width), BF),
            pltpu.VMEM((rows + 16, n * width), BF),
            pltpu.SemaphoreType.DMA((n,)),
            pltpu.SemaphoreType.DMA((3, n)),
        ],
        compiler_params=pltpu.CompilerParams(vmem_limit_bytes=VMEM),
        cost_estimate=TINY,
        name="early_qkv",
    )(idx, *x_list, w, mod)


def late_qkv(idx, x_list, w, acc, stat, mod, gain):
    rows, width = stat.shape[1], x_list[0].shape[1]
    n = len(x_list) + 1
    first = mod.shape[0] - n
    tile = rows // 2
    hbm = pl.BlockSpec(memory_space=pltpu.HBM)
    vmem = pl.BlockSpec(memory_space=pltpu.VMEM)
    return pl.pallas_call(
        functools.partial(
            late_kernel, first=first, tile=tile, scale=query_scale(gain.shape[1])
        ),
        in_specs=[pl.BlockSpec(memory_space=pltpu.SMEM)] + [hbm] * (n + 1) + [vmem] * 3,
        out_specs=[vmem] * 2,
        out_shape=[
            jax.ShapeDtypeStruct((rows, width), BF),
            jax.ShapeDtypeStruct((2, rows, width), BF),
        ],
        scratch_shapes=[
            pltpu.VMEM((n, rows, width), BF),
            pltpu.VMEM((n * width, 3 * width), BF),
            pltpu.VMEM(acc.shape, F32),
            pltpu.VMEM((rows, n * width), BF),
            pltpu.SemaphoreType.DMA((2, n)),
            pltpu.SemaphoreType.DMA((3, n)),
            pltpu.SemaphoreType.DMA,
        ],
        compiler_params=pltpu.CompilerParams(vmem_limit_bytes=VMEM),
        cost_estimate=TINY,
        name="late_qkv",
    )(idx, *x_list, w, acc, stat, mod, gain)


def text_qkv_kernel(idx_ref, *refs, blocks, scale):
    x_refs = list(refs[: blocks - 2]) + [refs[blocks - 2].at[0], refs[blocks - 2].at[1]]
    w_ref, mod_ref, gain_ref, out_ref, mod_buf = refs[blocks - 1 :]
    width = x_refs[0].shape[1]
    vals = [r[...].astype(F32) for r in x_refs]
    _, vals, square = moments(vals, gain_ref.shape[1])
    inverse = lax.rsqrt(square * (1.0 / (blocks * width)) + EPS_NORM)
    for n, v in enumerate(vals):
        m = mod_ref[idx_ref[n]]
        out = (v * inverse * (1.0 + m[1:2]) + m[0:1]).astype(BF)
        mod_buf[:, pl.ds(pl.multiple_of(idx_ref[n] * width, 128), width)] = out
    mixed = [jnp.dot(mod_buf[...], w_ref[p], preferred_element_type=F32) for p in range(3)]
    out_ref[:, :width] = rms_heads(mixed[0], gain_ref[0:1] * scale)
    out_ref[:, width : 2 * width] = rms_heads(mixed[1], gain_ref[1:2])
    out_ref[:, 2 * width :] = mixed[2].astype(BF)


def text_qkv(idx, x_list, w, mod, gain, rows):
    total, width = x_list[0].shape
    n = len(x_list) + 1
    last = total // rows - 1
    vmem = pl.BlockSpec(memory_space=pltpu.VMEM)
    return pl.pallas_call(
        functools.partial(text_qkv_kernel, blocks=n, scale=query_scale(gain.shape[1])),
        grid=(1,),
        in_specs=[pl.BlockSpec(memory_space=pltpu.SMEM)]
        + [pl.BlockSpec((rows, width), lambda i: (last, 0))] * (n - 2)
        + [pl.BlockSpec((2, rows, width), lambda i: (0, last, 0))]
        + [vmem] * 3,
        out_specs=vmem,
        out_shape=jax.ShapeDtypeStruct((rows, 3 * width), BF),
        scratch_shapes=[pltpu.VMEM((rows, n * width), BF)],
        compiler_params=pltpu.CompilerParams(vmem_limit_bytes=24 * 2**20),
        cost_estimate=cost(2),
        name="text_qkv",
    )(idx, *[in_hbm(x) for x in x_list], w, mod, gain)


def one(q, k, v, valid=None):
    s = lax.dot_general(q, k, (((1,), (1,)), ((), ())), preferred_element_type=F32)
    e = jnp.exp2(s)
    if valid is not None:
        e = jnp.where(lax.broadcasted_iota(jnp.int32, e.shape, 1) < valid, e, 0.0)
    hd = v.shape[1]
    wide = jnp.concatenate([v, jnp.ones_like(v)], axis=1)
    both = jnp.dot(e.astype(BF), wide, preferred_element_type=F32)
    return both[:, :hd], both[:, hd:]


def att_kernel(pos_ref, *refs, plan, n_q, n_kv, text, acc, packed):
    refs = list(refs)
    length = refs.pop(0) if text else None
    qs = [refs.pop(0) for _ in range(n_q)]
    kvs = [refs.pop(0) for _ in range(n_kv)]
    txt = [refs.pop(0) for _ in range(2)] if text else None
    accs = [refs.pop(0) for _ in range(2 * n_q)] if acc else None
    for i in range(n_q):
        num = accs[2 * i][...] if acc else None
        den = accs[2 * i + 1][...] if acc else None
        q = qs[i][...]
        parts = [(kvs[j].at[0], kvs[j].at[1], None) for j in plan[i]]
        if text and i == 0:
            parts.append((txt[0], txt[1], length[0]))
        for k_ref, v_ref, valid in parts:
            n, d = one(q, k_ref[...], v_ref[...], valid)
            num = n if num is None else num + n
            den = d if den is None else den + d
        if i in packed:
            out = refs.pop(0)
            out[0] = num.astype(BF)
            out[1] = den.astype(BF)
        else:
            refs.pop(0)[...] = num
            refs.pop(0)[...] = den


def attention(pos, qs, kvs, plan, text=None, acc=None, packed=(), name="att"):
    rows, width = qs[0].shape
    hd = 128
    heads = width // hd
    n_q = len(qs)
    args, specs = [], []
    if text is not None:
        args.append(text[0])
        specs.append(pl.BlockSpec(memory_space=pltpu.SMEM))
    q_spec = pl.BlockSpec((rows, hd), lambda h, p: (0, h))
    out_spec = pl.BlockSpec((rows, hd), lambda h, p: (0, h))
    for q in qs:
        args.append(q)
        specs.append(q_spec)
    keys = 0
    for kv in kvs:
        keys = kv.shape[1]
        specs.append(pl.BlockSpec((2, keys, hd), lambda h, p: (0, 0, h)))
        args.append(kv)
    if text is not None:
        tk = text[1]
        args += [tk, tk]
        specs.append(pl.BlockSpec((tk.shape[0], hd), lambda h, p: (0, heads + h)))
        specs.append(pl.BlockSpec((tk.shape[0], hd), lambda h, p: (0, 2 * heads + h)))
    if acc is not None:
        args += list(acc)
        specs += [q_spec] * len(acc)
    outs, out_specs = [], []
    for i in range(n_q):
        if i in packed:
            outs.append(jax.ShapeDtypeStruct((2, rows, width), BF))
            out_specs.append(pl.BlockSpec((2, rows, hd), lambda h, p: (0, 0, h)))
        else:
            outs += [jax.ShapeDtypeStruct((rows, width), F32)] * 2
            out_specs += [out_spec] * 2
    blocks = sum(len(p) for p in plan)
    return pl.pallas_call(
        functools.partial(
            att_kernel, plan=plan, n_q=n_q, n_kv=len(kvs), text=text is not None, acc=acc is not None, packed=packed
        ),
        grid_spec=pltpu.PrefetchScalarGridSpec(
            num_scalar_prefetch=1, grid=(heads,), in_specs=specs, out_specs=out_specs
        ),
        out_shape=outs,
        compiler_params=pltpu.CompilerParams(vmem_limit_bytes=VMEM),
        cost_estimate=pl.CostEstimate(
            flops=14 * rows * keys * width * blocks, bytes_accessed=1, transcendentals=0
        ),
        name=name,
    )(pos, *args)


def text_att_kernel(q_ref, kv_ref, out_ref):
    n_patch, _, rows, width = out_ref.shape
    hd = 128
    for h in range(width // hd):
        cols = slice(h * hd, (h + 1) * hd)
        num, den = one(q_ref[:, cols], kv_ref[0, :, cols], kv_ref[1, :, cols])
        out_ref[:, 0, :, cols] = num.astype(BF).reshape(n_patch, rows, hd)
        out_ref[:, 1, :, cols] = den.astype(BF).reshape(n_patch, rows, hd)


def text_attention(txt, kv, n_patch):
    rows = txt.shape[0]
    width = kv.shape[2]
    return pl.pallas_call(
        text_att_kernel,
        grid=(1,),
        in_specs=[pl.BlockSpec((rows, width), lambda i: (0, 0)), pl.BlockSpec(kv.shape, lambda i: (0, 0, 0))],
        out_specs=pl.BlockSpec((n_patch, 2, rows // n_patch, width), lambda i: (0, 0, 0, 0)),
        out_shape=jax.ShapeDtypeStruct((n_patch, 2, rows // n_patch, width), BF),
        compiler_params=pltpu.CompilerParams(vmem_limit_bytes=VMEM),
        cost_estimate=cost(3),
        name="text_attention",
    )(txt, kv)


def text_keys(q_ref, txt_ref, len_ref, h):
    hd = 128
    width = q_ref.shape[1]
    at = h * hd
    k = txt_ref[:, width + at : width + at + hd]
    v = txt_ref[:, 2 * width + at : 2 * width + at + hd]
    return one(q_ref[:, at : at + hd], k, v, len_ref[0])


def image_quotient(len_ref, q_ref, k_ref, v_ref, num_ref, den_ref, got_ref, attn_ref):
    n, d = one(q_ref[...], k_ref[...], v_ref[...], len_ref[0])
    num = n + num_ref[...] + got_ref[0].astype(F32)
    den = d + den_ref[...] + got_ref[1].astype(F32)
    attn_ref[...] = (num / den).astype(BF)


def quotient(text_len, q, txt, num, den, got):
    rows, width = q.shape
    keys = txt.shape[0]
    hd = 128
    heads = width // hd
    part = pl.BlockSpec((rows, hd), lambda h: (0, h))
    return pl.pallas_call(
        image_quotient,
        grid=(heads,),
        in_specs=[
            pl.BlockSpec(memory_space=pltpu.SMEM),
            part,
            pl.BlockSpec((keys, hd), lambda h: (0, heads + h)),
            pl.BlockSpec((keys, hd), lambda h: (0, 2 * heads + h)),
            part,
            part,
            pl.BlockSpec((2, rows, hd), lambda h: (0, 0, h)),
        ],
        out_specs=part,
        out_shape=jax.ShapeDtypeStruct(q.shape, BF),
        compiler_params=pltpu.CompilerParams(vmem_limit_bytes=VMEM),
        cost_estimate=cost(4),
        name="quotient",
    )(text_len, q, txt, txt, num, den, got)


def text_quotient_kernel(len_ref, sum_ref, q_ref, txt_ref, proj_ref, out_ref):
    rows, width = q_ref.shape
    hd = 128
    parts = []
    for h in range(width // hd):
        cols = slice(h * hd, (h + 1) * hd)
        n, d = text_keys(q_ref, txt_ref, len_ref, h)
        num = n + jnp.sum(sum_ref[:, 0, :, cols].astype(F32), axis=0)
        den = d + jnp.sum(sum_ref[:, 1, :, cols].astype(F32), axis=0)
        parts.append((num / den).astype(BF))
    attn = jnp.concatenate(parts, axis=1)
    part = jnp.dot(attn, proj_ref[...], preferred_element_type=F32).astype(BF)
    for j in range(out_ref.shape[0]):
        out_ref[j] = part[:, j * width : (j + 1) * width]


def text_quotient(text_len, sums, q, txt, proj, n_head):
    vmem = pl.BlockSpec(memory_space=pltpu.VMEM)
    return pl.pallas_call(
        text_quotient_kernel,
        in_specs=[pl.BlockSpec(memory_space=pltpu.SMEM)] + [vmem] * 4,
        out_specs=vmem,
        out_shape=jax.ShapeDtypeStruct((n_head,) + q.shape, BF),
        compiler_params=pltpu.CompilerParams(vmem_limit_bytes=VMEM),
        cost_estimate=cost(4),
        name="text_quotient",
    )(text_len, sums, q, txt, proj)


def proj_kernel(pos_ref, mine_ref, got_ref, w_ref, wz_ref, wc_ref, *refs):
    outs = refs[:NY]
    w_buf, sem = refs[NY:]
    width = mine_ref.shape[1]
    zh, y, core = pos_ref[0], pos_ref[1], pos_ref[2]
    half = width // 2
    order = (2, 1, 3, 0)

    def copies(d):
        block = lax.rem(y + d, NY)
        sources = (
            (w_ref, zh * NY + block, 0, width),
            (wz_ref, block, width + core * half, half),
            (wc_ref, block, width + (1 - core) * half, half),
        )
        return [
            pltpu.make_async_copy(
                ref.at[:, pl.ds(pl.multiple_of(at * width, 128), width)],
                w_buf.at[d, pl.ds(row if i == 0 else pl.multiple_of(row, half), size)],
                sem.at[d, i],
            )
            for i, (ref, at, row, size) in enumerate(sources)
        ]

    for d in order:
        for copy in copies(d):
            copy.start()
    both = jnp.concatenate([mine_ref[...], got_ref[...]], axis=1)
    for d in order:
        for copy in copies(d):
            copy.wait()
        outs[d][...] = jnp.dot(both, w_buf[d], preferred_element_type=F32).astype(BF)


def project(pos, mine, got, w, wz, wc):
    width = mine.shape[1]
    spec = pl.BlockSpec(memory_space=pltpu.VMEM)
    hbm = pl.BlockSpec(memory_space=pltpu.HBM)
    return pl.pallas_call(
        proj_kernel,
        in_specs=[pl.BlockSpec(memory_space=pltpu.SMEM)] + [spec] * 2 + [hbm] * 3,
        out_specs=[spec] * NY,
        out_shape=[jax.ShapeDtypeStruct(mine.shape, BF)] * NY,
        scratch_shapes=[
            pltpu.VMEM((NY, 2 * width, width), BF),
            pltpu.SemaphoreType.DMA((NY, 3)),
        ],
        compiler_params=pltpu.CompilerParams(vmem_limit_bytes=VMEM),
        cost_estimate=cost(6),
        name="project",
    )(pos, mine, got, w, wz, wc)


def exchange(parts):
    total = parts[0].astype(F32)
    for d in range(1, NY):
        total = total + send_head(parts[d], dy=d).astype(F32)
    return total


def shards(
    image,
    text,
    text_len,
    img_mod,
    txt_mod,
    img_qkv,
    txt_qkv,
    img_proj,
    txt_proj,
    img_gain,
    txt_gain,
    stale_kv,
):
    n_head = lax.axis_size("head")
    n_patch = lax.axis_size("patch")
    me_h = lax.axis_index("head")
    me_p = lax.axis_index("patch")
    zh, y = me_h // NY, me_h % NY
    group, width = image.shape
    txt_total = text.shape[0]
    t_rows = txt_total // n_patch

    pos = jnp.stack([zh, y, me_p % 2]).astype(jnp.int32)

    t_own = lax.dynamic_slice_in_dim(text, me_p * t_rows, t_rows, 0)
    rows = jnp.concatenate([image, t_own], axis=0)
    i_z = send_head(rows, dz=1)
    i_m = send_head(rows, dy=1)
    i_p = send_head(rows, dy=-1)
    kv_m = send_patch(stale_kv, dx=1)
    core = me_p % 2
    part_z = lax.dynamic_slice(
        img_proj, (core * (width // 2), (1 - zh) * NY * width), (width // 2, NY * width)
    )
    near = after(i_z, i_m, i_p, part_z)
    ahead = send_head(jnp.stack([i_m, near]), dy=1)
    iz_p = send_head(near, dy=-1)
    mod_i = img_mod.reshape(3, n_head, width).transpose(1, 0, 2)
    mod_t = txt_mod.reshape(3, n_head, width).transpose(1, 0, 2)
    ring = (y + jnp.array([0, 0, NY - 1, 1, 1, 2, 2, NY - 1])) % NY
    side = (zh + jnp.array([0, 1, 0, 0, 1, 1, 0, 1])) % 2
    idx = (side * NY + ring).astype(jnp.int32)
    w_i = img_qkv.transpose(1, 0, 2)
    iz_2 = send_head(iz_p, dy=-1)
    acc, stat = early_qkv(after(idx, kv_m, iz_p), [rows, near, i_m, i_p], w_i, mod_i, group)
    later = after(stale_kv, iz_p)
    kv_z = send_patch(later, dz=1)
    kv_p = send_patch(later, dx=-1)
    kv_2 = send_patch(kv_m, dx=1)
    kvz_m = send_patch(kv_z, dx=1)
    kvz_p = send_patch(kv_z, dx=-1)
    kvz_2 = send_patch(kv_2, dz=1)
    proj_z = send_head(after(part_z, kv_z), dz=1)
    proj_c = send_patch(proj_z, dc=1)
    q, kv = late_qkv(idx, [iz_p, iz_2, ahead], w_i, acc, stat, mod_i, img_gain)
    x_list = [rows, near, i_m, i_p, iz_p, iz_2, ahead]
    q_c = send_patch(q, dc=1)
    t_pack = text_qkv(after(idx, q), x_list, txt_qkv.transpose(1, 0, 2), mod_t, txt_gain, t_rows)
    t_q = t_pack[:, :width]
    txt = lax.all_to_all(
        jnp.broadcast_to(t_pack[None], (n_patch,) + t_pack.shape), "patch", 0, 0
    ).reshape(txt_total, 3 * width)

    both = attention(
        after(pos, t_pack),
        [q, q_c],
        [kv, stale_kv, kv_m, kv_p, kv_2, kv_z],
        [[0, 2, 3, 4, 5], [1, 2, 3, 4, 5]],
        name="att_near",
    )
    t_sums = text_attention(after(txt, both[0]), kv, n_patch)
    t_got = lax.all_to_all(t_sums, "patch", 0, 0)
    num, den, part_c = attention(
        after(pos, t_sums),
        [q, q_c],
        [kvz_m, kvz_p, kvz_2],
        [[0, 1, 2]] * 2,
        acc=both,
        packed=(1,),
        name="att_last",
    )
    got_c = send_patch(part_c, dc=1)
    attn = quotient(text_len, q, txt, num, den, after(got_c, proj_c))
    from_z = send_head(attn, dz=1)
    t_proj = text_quotient(text_len, after(t_got, attn), t_q, txt, txt_proj, n_head)
    img_sum = exchange(project(pos, attn, from_z, img_proj, proj_z, proj_c))
    column = me_h * width
    img_gate = lax.dynamic_slice_in_dim(img_mod[2], column, width)
    img_out = (image.astype(F32) + img_gate * img_sum).astype(BF)
    t_sum = lax.all_to_all(t_proj, "head", 0, 0).astype(F32).sum(axis=0)
    txt_gate = lax.dynamic_slice_in_dim(txt_mod[2], column, width)
    t_out = (t_own.astype(F32) + txt_gate * t_sum).astype(BF)
    txt_out = lax.all_to_all(
        jnp.broadcast_to(t_out[None], (n_patch,) + t_out.shape), "patch", 0, 0
    ).reshape(txt_total, width)
    return (img_out, txt_out)


def solution(mesh):
    in_specs = (
        P("patch", "head"),
        P(None, "head"),
        P(),
        P(),
        P(),
        P(None, None, "head"),
        P(None, None, "head"),
        P("head", None),
        P("head", None),
        P(),
        P(),
        P(None, "patch", "head"),
    )
    out_specs = (P("patch", "head"), P(None, "head"))
    return jax.shard_map(shards, mesh=mesh, in_specs=in_specs, out_specs=out_specs, check_vma=False)
```
